256 devices in a mesh: ctx: 32 (over y, z_lo, x), head: 8 (over z_hi, core).
Axes of the slice: x: 4, y: 4, z: 8 (z_hi: 4, z_lo: 2; z = z_hi * 2 + z_lo), core: 2. Of those that a mesh axis runs over, the one named last changes fastest.
Arguments:
- q_nope: bfloat16 [4096, 8192], P('ctx', 'head'), may hold values from -210 to 210
- q_rope: bfloat16 [4096, 4096], P('ctx', 'head'), may hold values from -6 to 6
- key_latent: bfloat16 [4096, 576], P(('ctx', 'head')), may hold values from -6 to 6
- doc_ids: int32 [4096], P(('ctx', 'head')), may hold values from 0 to 3, as said below
- doc_offsets: int32 [4], replicated, may hold values from 0 to 98303
- owners: int32 [4096, 1], P(('ctx', 'head')), may hold values from 0 to 31; in each aligned block of 128 rows (0 to 127, 128 to 255, ...) at most 8 rows name the same one
- w_key: bfloat16 [64, 128, 512], P('head'), may hold values from -0.5 to 0.5
- w_value: bfloat16 [64, 512, 128], P('head'), may hold values from -0.25 to 0.25
Outputs:
- attended: bfloat16 [4096, 8192], P('ctx', 'head')
- cache: bfloat16 [8192, 576], P(('ctx', 'head'))
The draws below stay inside these ranges and needn't reach their ends.
Inputs may be any that keep to these rules, and one draw needn't show every extreme that they name: `doc_ids`: never falls; request 0 has exactly 2056 tokens, every other request 1 or more. `owners`: in each aligned block of 128 rows no owner is named by more than 8 rows; in some block some owner is named by exactly 8.
All inputs are finite; a program needn't handle non-finite values.
Results may differ from the reference program's by a relative error of at most 0.011.
Values may be sent and summed in bfloat16 or wider, within the bound.
A program may use at most 64 MiB of HBM per device.

```python
import math
import jax
import jax.numpy as jnp
import numpy as np
from jax import lax

H = 64
NOPE = 128
ROPE = 64
LATENT = 512
VDIM = 128
REQS = 4
T_DEV = 128
S = 4096
SLOTS = 1
CAP = 8
CACHE = 8192
DOC_MOST = 2056
N_CTX = 32
N_HEAD = 8


def draw_q_nope(key, part):
    key = jax.random.fold_in(key, 11)
    first_key = jax.random.fold_in(key, 0)
    return jax.random.truncated_normal(first_key, -6.0, 6.0, (S, H * NOPE), jnp.float32).astype(jnp.bfloat16)


def draw_doc_ids(key, part):
    key = jax.random.fold_in(key, 5)
    span = S - DOC_MOST - 1
    picks = jax.random.permutation(key, span)[:REQS - 2].astype(jnp.int32) + DOC_MOST + 1
    cuts = jnp.sort(picks)
    rows = jnp.arange(S, dtype=jnp.int32)
    later = jnp.sum((rows[:, None] >= cuts[None, :]).astype(jnp.int32), 1)
    return (rows >= DOC_MOST).astype(jnp.int32) + later


def with_ends(array, stream_key, smallest, largest):
    longest = array.shape.index(max(array.shape))
    spots = []
    for shift in (0, 1):
        where = [jax.random.randint(jax.random.fold_in(stream_key, axis), (), 0, length) for axis, length in enumerate(array.shape)]
        where[longest] = (where[longest] + shift) % array.shape[longest]
        spots.append(tuple(where))
    return array.at[spots[0]].set(smallest).at[spots[1]].set(largest)


def level_of(rng, dims, pieces, least, largest):
    def one(dim, blocks):
        draws = jax.random.uniform(jax.random.fold_in(jax.random.fold_in(rng, 6), dim), (blocks,), jnp.float32, least / len(pieces), largest / len(pieces))
        return jnp.repeat(jnp.exp(draws), dims[dim] // blocks).reshape((-1,) + (1,) * (len(dims) - dim - 1))

    loudness = one(*pieces[0])
    for cut in pieces[1:]:
        loudness = loudness * one(*cut)
    return loudness


def shared_out(own_key, own, number, rows, number_of, top, bound, lean):
    sequence = jax.random.permutation(own_key, number_of)
    heavy_load, common = load_shares(number_of, rows * top, bound, lean, True), load_shares(number_of, rows * top, bound, lean, False)
    places = jnp.arange(number_of)

    def named(sizes, offset_by):
        used = int((sizes > 0).sum())
        fixed = max(1, used // 4)
        moved = fixed + (places - fixed + offset_by * (used - fixed)) % max(1, number_of - fixed)
        return jnp.zeros((number_of,), jnp.int32).at[sequence[jnp.where(places < fixed, places, moved)]].set(jnp.asarray(sizes, jnp.int32))

    sizes = jnp.where(number % 4 == 0, named(heavy_load, number // 4), named(common, number - number // 4 - 1))
    mixed = jax.random.permutation(jax.random.fold_in(own, 3), number_of)
    source_of, receiver = mixed[0:number_of // 2 * 2:2], mixed[1:number_of // 2 * 2:2]
    slack = jnp.minimum(sizes[source_of] - 1, bound - sizes[receiver]) // 2
    slack = jnp.where((source_of == sequence[0]) | (receiver == sequence[0]) | (sizes[receiver] == 0), 0, jnp.maximum(slack, 0))
    moved = jax.random.randint(jax.random.fold_in(own, 4), (number_of // 2,), 0, 1 << 20) % (slack + 1)
    sizes = sizes.at[source_of].add(-moved).at[receiver].add(moved)
    labels = jnp.searchsorted(jnp.cumsum(sizes), jnp.arange(rows * top), side="right").astype(jnp.int32)
    grid = labels.reshape(top, rows).T
    grid = grid[jax.random.permutation(jax.random.fold_in(own, 1), rows)]
    offset_by = jax.random.randint(jax.random.fold_in(own, 2), (rows, 1), 0, top)
    return jnp.take_along_axis(grid, (jnp.arange(top)[None, :] + offset_by) % top, axis=1)


def load_shares(count, total, reach, lean, full):
    portions = [(1 << 20) // math.isqrt(rank ** lean) + 1 for rank in range(1, count + 1)]
    largest = reach if full else min(reach, max(-(-total // count), total * portions[0] // sum(portions)))
    least = 1 if total - largest >= count - 1 else 0
    given, rest = [largest] + [least] * (count - 1), total - largest - least * (count - 1)
    while rest > 0:
        candidates = [i for i in range(1, count) if given[i] < largest] or [i for i in range(1, count) if given[i] < reach]
        whole, remaining = sum([portions[i] for i in candidates]), rest
        for i in candidates:
            addition = min(reach - given[i], max(1, remaining * portions[i] // whole), rest)
            given[i] = given[i] + addition
            rest = rest - addition
    return np.array(given)


def noise(key, dims, deviation, reach, pieces=(), kind=jnp.bfloat16):
    array = deviation * jax.random.normal(key, dims, jnp.float32)
    if pieces:
        array = array * level_of(key, dims, pieces, -0.22, 0.18)
    return jnp.clip(array, -reach, reach).astype(kind)


def setup_inputs(seed: int = 0) -> dict:
    key_of = jax.random.split(jax.random.key(seed), 9)
    q_nope = draw_q_nope(jax.random.fold_in(key_of[8], 71), 0)
    q_rope = noise(key_of[1], (S, H * ROPE), 1.0, 6.0, ((0, 32), (1, 8)))
    key_latent = noise(key_of[2], (S, LATENT + ROPE), 1.0, 6.0, ((0, 256),))
    doc_ids = draw_doc_ids(jax.random.fold_in(key_of[8], 71), 0)
    doc_offsets = with_ends(jax.random.randint(key_of[4], (REQS,), 0, 98304), jax.random.fold_in(key_of[4], 1), 0, 98303).astype(jnp.int32)
    owners_keys = jax.random.split(jax.random.fold_in(key_of[5], 1), S // T_DEV)
    owners_turns = jax.random.permutation(jax.random.fold_in(key_of[5], 3), S // T_DEV)
    owners = jax.vmap(lambda own, number: shared_out(jax.random.fold_in(key_of[5], 2), own, number, T_DEV, N_CTX, 1, CAP, 2))(owners_keys, owners_turns).reshape((S, 1))
    w_key = noise(key_of[6], (H, NOPE, LATENT), NOPE ** -0.5, 0.5, ((0, 8),))
    w_value = noise(key_of[7], (H, LATENT, VDIM), LATENT ** -0.5, 0.25, ((0, 8),))
    return dict(q_nope=q_nope, q_rope=q_rope, key_latent=key_latent, doc_ids=doc_ids, doc_offsets=doc_offsets, owners=owners, w_key=w_key, w_value=w_value)


def rotate(values, positions):
    half = values.shape[-1] // 2
    steps = jnp.arange(half, dtype=jnp.float32)
    inverse = 10000.0 ** (-2.0 * steps / values.shape[-1])
    angle = positions.astype(jnp.float32)[..., None] * inverse
    first = values[..., :half]
    second = values[..., half:]
    cosine = jnp.cos(angle)
    sine = jnp.sin(angle)
    return jnp.concatenate([first * cosine - second * sine, first * sine + second * cosine], -1)


def dispatch(targets, values):
    hits = (targets[:, None] == jnp.arange(N_CTX, dtype=jnp.int32)[None, :]).astype(jnp.int32)
    slots = jnp.cumsum(hits, 0) - hits
    place = (hits[:, :, None] == 1) & (slots[:, :, None] == jnp.arange(CAP, dtype=jnp.int32)[None, None, :])
    return jnp.einsum('rnc,rd->ncd', place.astype(jnp.float32), values.astype(jnp.float32)).astype(jnp.bfloat16)


def reference(q_nope, q_rope, key_latent, doc_ids, doc_offsets, owners, w_key, w_value):
    rows = jnp.arange(S, dtype=jnp.int32)
    starts = jnp.sum((doc_ids[None, :] < jnp.arange(REQS, dtype=jnp.int32)[:, None]).astype(jnp.int32), 1)
    positions = doc_offsets[doc_ids] + rows - starts[doc_ids]
    rope_keys = rotate(key_latent[:, LATENT:].astype(jnp.float32), positions).astype(jnp.bfloat16)
    key_rows = jnp.concatenate([key_latent[:, :LATENT], rope_keys], 1)
    nope = q_nope.reshape(S, H, NOPE).astype(jnp.float32)
    absorbed = jnp.einsum('thd,hdc->thc', nope, w_key.astype(jnp.float32)).astype(jnp.bfloat16)
    rotated = rotate(q_rope.reshape(S, H, ROPE).astype(jnp.float32), positions[:, None]).astype(jnp.bfloat16)
    query = jnp.concatenate([absorbed, rotated], 2)
    keys_wide = key_rows.astype(jnp.float32)
    scale = (NOPE + ROPE) ** -0.5

    def block(index):
        first = index * T_DEV
        q_block = lax.dynamic_slice_in_dim(query, first, T_DEV, 0).astype(jnp.float32)
        q_docs = lax.dynamic_slice_in_dim(doc_ids, first, T_DEV, 0)
        q_rows = first + jnp.arange(T_DEV, dtype=jnp.int32)
        scores = jnp.einsum('thc,kc->thk', q_block, keys_wide) * scale
        mask = ((q_docs[:, None] == doc_ids[None, :]) & (rows[None, :] <= q_rows[:, None]))[:, None, :]
        highest = jnp.max(jnp.where(mask, scores, -1e30), 2, keepdims=True)
        weights = jnp.where(mask, jnp.exp(scores - highest), 0.0)
        total = jnp.sum(weights, 2)
        rounded = lax.optimization_barrier(weights.astype(jnp.bfloat16))
        mixed = jnp.einsum('thk,kc->thc', rounded.astype(jnp.float32), keys_wide[:, :LATENT])
        latent_out = lax.optimization_barrier((mixed / total[..., None]).astype(jnp.bfloat16))
        result = jnp.einsum('thc,hcd->thd', latent_out.astype(jnp.float32), w_value.astype(jnp.float32))
        return result.astype(jnp.bfloat16).reshape(T_DEV, H * VDIM)

    attended = lax.map(block, jnp.arange(N_CTX, dtype=jnp.int32)).reshape(S, H * VDIM)
    owner_rows = owners[:, 0].reshape(N_CTX, T_DEV)
    group_rows = key_rows.reshape(N_CTX, T_DEV, LATENT + ROPE)
    buffers = jax.vmap(dispatch)(owner_rows, group_rows)
    buffers = buffers.reshape(N_CTX, N_CTX, N_HEAD, SLOTS, LATENT + ROPE)
    cache = jnp.transpose(buffers, (1, 2, 0, 3, 4)).reshape(CACHE, LATENT + ROPE)
    return attended, cache
```

```python
import functools

import jax
import jax.numpy as jnp
import numpy as np
from jax import lax
from jax.experimental import pallas as pl
from jax.experimental.pallas import tpu as pltpu
from jax.sharding import PartitionSpec as P

NOPE = 128
ROPE = 64
LATENT = 512
VDIM = 128
HEADS = 8
TOK = 128
HALF = 64
WIDE = 640
STRIP = 16
TILE = 256
BIG = float(2.0**100)
DEAD = -1e30
SCALE = (NOPE + ROPE) ** -0.5 * 1.4426950408889634
INVERSE = [float(v) for v in (10000.0 ** (-2.0 * np.arange(32) / 64.0)).astype(np.float32)]
DOC = 64
GONE = 68
NAT = 69
OWNER = 70
COUNT = 72
BLOCK = 80

MESH = pl.DeviceIdType.MESH
NT = (((1,), (1,)), ((), ()))
NN = (((1,), (0,)), ((), ()))


def iota(shape, dim):
    return lax.broadcasted_iota(jnp.int32, shape, dim)


def place(y, zl, x, zh, core):
    return (lax.rem(y, 4) * 8 + lax.rem(zl, 2) * 4 + lax.rem(x, 4), lax.rem(zh, 4) * 2 + core)


def inverse_lanes(shape):
    index = lax.rem(iota(shape, 1), 32)
    out = jnp.zeros(shape, jnp.float32)
    for j, value in enumerate(INVERSE):
        out = jnp.where(index == j, value, out)
    return out


def cos_sin(angle):
    turns = jnp.floor(angle * 0.6366197723675814 + 0.5)
    rest = angle - turns * 1.5703125
    rest = rest - turns * 4.837512969970703125e-4
    rest = rest - turns * 7.54978995489188216e-8
    z = rest * rest
    sine = rest + rest * z * (
        -1.6666654611e-1 + z * (8.3321608736e-3 - z * 1.9515295891e-4)
    )
    cosine = 1.0 - 0.5 * z + z * z * (
        4.166664568298827e-2 + z * (-1.388731625493765e-3 + z * 2.443315711809948e-5)
    )
    quadrant = turns.astype(jnp.int32) & 3
    swap = (quadrant & 1) == 1
    c = jnp.where(swap, sine, cosine)
    s = jnp.where(swap, cosine, sine)
    c = jnp.where((quadrant == 1) | (quadrant == 2), -c, c)
    s = jnp.where(quadrant >= 2, -s, s)
    return c, s


def turn(values, cosine, signed_sine):
    first = lax.rem(iota(values.shape, 1), 64) < 32
    partner = jnp.where(first, pltpu.roll(values, 96, 1), pltpu.roll(values, 32, 1))
    return values * cosine + partner * signed_sine


def sign_sine(sine):
    return jnp.where(lax.rem(iota(sine.shape, 1), 64) < 32, -sine, sine)


def nat_of(k):
    return lax.div(lax.rem(k, 64), 16) * 32 + lax.div(k, 64) * 16 + lax.rem(k, 16)


def kernel(
    qn_hbm, qr_hbm, kl_hbm, doc_ref, off_ref, own_hbm, wk_hbm, wv_hbm,
    out_ref, cache_ref,
    qn, qr, kl, own, wk, wv, raw, keys, query, acc, top, total, mask, cos_t, sin_t,
    s1, r1, s2, r2, hq_out, hq, hacc, htop, htotal, hout, hin,
    local_sem, pa_send, pa_recv, raw_send, raw_recv, m_send, m_recv, sib_send, sib_recv,
    c1_send, c1_recv, c2_send, c2_recv, h_send, h_recv,
):
    ctx = lax.axis_index("ctx")
    head = lax.axis_index("head")
    y, zl, x = lax.div(ctx, 8), lax.rem(lax.div(ctx, 4), 2), lax.rem(ctx, 4)
    zh, core = lax.div(head, 2), lax.rem(head, 2)
    odd = lax.rem(y, 2) == 1
    even = lax.rem(y, 2) == 0
    lane_group = zl * 4 + x

    z_up = lax.rem(zh * 2 + zl + 1, 8)
    z_down = lax.rem(zh * 2 + zl + 7, 8)
    to_z_up = place(y, lax.rem(z_up, 2), x, lax.div(z_up, 2), core)
    to_z_down = place(y, lax.rem(z_down, 2), x, lax.div(z_down, 2), core)
    to_x_up = place(y, zl, x + 1, zh, core)
    to_x_down = place(y, zl, x + 3, zh, core)
    to_y_up = place(y + 1, zl, x, zh, core)
    sibling = (ctx, zh * 2 + 1 - core)
    z_peers = [place(y, zl, x, zh + d, core) for d in (1, 2, 3)]
    y_peers = [place(y + d, zl, x, zh, core) for d in (1, 2, 3)]
    group_peers = []
    for d in range(1, 8):
        j = lax.rem(lane_group + d, 8)
        group_peers.append(place(y, lax.div(j, 4), lax.rem(j, 4), zh, core))
    other_zh = zh + zl * 2 + 3
    other_z = place(y, zl + 1, x, other_zh, core)

    locals_ = [
        pltpu.make_async_copy(kl_hbm, kl, local_sem.at[0]),
        pltpu.make_async_copy(own_hbm, own, local_sem.at[1]),
        pltpu.make_async_copy(qr_hbm, qr, local_sem.at[2]),
        pltpu.make_async_copy(qn_hbm, qn, local_sem.at[3]),
        pltpu.make_async_copy(wk_hbm, wk, local_sem.at[4]),
        pltpu.make_async_copy(wv_hbm, wv, local_sem.at[5]),
    ]
    for copy in locals_:
        copy.start()
    barrier = pltpu.get_barrier_semaphore()
    greeted = z_peers + y_peers + group_peers + [sibling, other_z]
    for peer in greeted:
        pl.semaphore_signal(barrier, inc=1, device_id=peer, device_id_type=MESH)

    lane128 = iota((TOK, 128), 1)

    @pl.when(even)
    def _():
        blank = jnp.where(iota((2 * HALF, 128), 1) == GONE, 1.0, 0.0).astype(jnp.bfloat16)
        blank = blank.reshape(2, HALF, 128)
        zero = jnp.zeros((2, HALF, LATENT), jnp.bfloat16)
        for s in (2, 6, 10, 14):
            keys[0, s : s + 2, :, :LATENT] = zero
            keys[0, s : s + 2, :, LATENT:] = blank
        for s in (8, 10, 12, 14):
            keys[1, s : s + 2, :, :LATENT] = zero
            keys[1, s : s + 2, :, LATENT:] = blank

    hq[TOK + STRIP :, :LATENT] = jnp.zeros((TOK - STRIP, LATENT), jnp.bfloat16)
    hq[TOK + STRIP :, LATENT:] = jnp.where(
        iota((TOK - STRIP, 128), 1) == GONE, 1.0, 0.0
    ).astype(jnp.bfloat16)
    inverse = inverse_lanes((8, 128))[0:1, :]
    token = (ctx * TOK + iota((TOK, 128), 0)).astype(jnp.float32)
    c, s = cos_sin(token * inverse)
    cos_t[...] = c
    sin_t[...] = sign_sine(s)
    for core_half in (0, 1):
        k = iota((TOK, 128), 1)
        dead = (k < 64) & (nat_of(core_half * 64 + lax.rem(k, 64)) > iota((TOK, 128), 0))
        mask[core_half] = jnp.where(dead, DEAD, 0.0)

    docs = jnp.zeros((STRIP, 128), jnp.int32)
    for r in range(STRIP):
        docs = jnp.where(iota((STRIP, 128), 0) == r, doc_ref[r], docs)
    lane = iota((STRIP, 128), 1)
    locals_[0].wait()
    locals_[1].wait()
    facts = jnp.where((lane == DOC + docs) | (lane == COUNT + docs), 1.0, 0.0)
    facts = jnp.where(lane == BLOCK + lax.rem(ctx, 16), 1.0, facts)
    facts = jnp.where(lane == NAT, (head * STRIP + iota((STRIP, 128), 0)).astype(jnp.float32), facts)
    facts = jnp.where(lane == OWNER, own[...].astype(jnp.float32), facts)
    mine = pl.ds(pl.multiple_of(zh * STRIP, STRIP), STRIP)
    raw[core, mine, :LATENT] = kl[:, :LATENT]
    raw[core, mine, LATENT:] = jnp.concatenate(
        [kl[:, LATENT:], facts[:, ROPE:].astype(jnp.bfloat16)], 1
    )
    pl.semaphore_wait(barrier, len(greeted))

    pa = [
        pltpu.make_async_remote_copy(
            src_ref=raw.at[core, mine], dst_ref=raw.at[core, mine],
            send_sem=pa_send.at[d], recv_sem=pa_recv.at[d],
            device_id=z_peers[d], device_id_type=MESH,
        )
        for d in range(3)
    ]
    for copy in pa:
        copy.start()

    locals_[2].wait()
    for pair in range(4):
        v = turn(qr[:, pair * 128 : pair * 128 + 128].astype(jnp.float32), cos_t[...], sin_t[...])
        base = pair * 2 * TOK
        query[base : base + TOK, LATENT:] = v.astype(jnp.bfloat16)
        query[base + TOK : base + 2 * TOK, LATENT:] = pltpu.roll(v, 64, 1).astype(jnp.bfloat16)
    locals_[3].wait()
    locals_[4].wait()
    for h in range(HEADS):
        a = lax.dot_general(
            qn[:, h * NOPE : (h + 1) * NOPE], wk[h], NN, preferred_element_type=jnp.float32
        )
        query[h * TOK : (h + 1) * TOK, :LATENT] = a.astype(jnp.bfloat16)

    plan = {0: [], 1: []}

    def send(scheme, src, dst, to, sem, half=None):
        a, b = keys.at[scheme, src], keys.at[scheme, dst]
        if half is not None:
            a, b = a.at[pl.ds(half * 32, 32)], b.at[pl.ds(half * 32, 32)]
        return pltpu.make_async_remote_copy(
            src_ref=a, dst_ref=b, send_sem=m_send.at[sem],
            recv_sem=m_recv.at[16 if half == 1 else dst], device_id=to, device_id_type=MESH,
        )

    def go(scheme, src, dst, to, half=None, cond=None, inside=None):
        number = len(plan[scheme])
        make = functools.partial(send, scheme, src, dst, to, number, half)
        plan[scheme].append((make, cond if inside is None else inside))
        if cond is None:
            make().start()
        else:
            @pl.when(cond)
            def _():
                make().start()

    def arrived(scheme, slot, half=None):
        ref = keys.at[scheme, slot]
        sem = slot
        if half is not None:
            ref = ref.at[pl.ds(half * 32, 32)]
            sem = 16 if half == 1 else slot
        pltpu.make_async_copy(ref, ref, m_recv.at[sem]).wait()

    def share(scheme, slot):
        return pltpu.make_async_remote_copy(
            src_ref=keys.at[scheme, slot], dst_ref=keys.at[scheme, slot],
            send_sem=sib_send.at[slot], recv_sem=sib_recv.at[slot],
            device_id=sibling, device_id_type=MESH,
        )

    def own_slot(half):
        v = raw[half, :, LATENT:].astype(jnp.float32)
        cc = jnp.concatenate([cos_t[n * 32 + half * 16 : n * 32 + half * 16 + 16, :] for n in range(4)], 0)
        ss = jnp.concatenate([sin_t[n * 32 + half * 16 : n * 32 + half * 16 + 16, :] for n in range(4)], 0)
        rotated = jnp.where(iota((HALF, 128), 1) < ROPE, turn(v, cc, ss), v)
        keys[half, 0, :, :LATENT] = raw[half, :, :LATENT]
        keys[half, 0, :, LATENT:] = rotated.astype(jnp.bfloat16)

    for d in range(3):
        pa[d].wait_recv()
    share_raw = pltpu.make_async_remote_copy(
        src_ref=raw.at[core], dst_ref=raw.at[core], send_sem=raw_send, recv_sem=raw_recv,
        device_id=sibling, device_id_type=MESH,
    )
    share_raw.start()

    on_a, on_b = core == 0, core == 1

    @pl.when(on_a)
    def _():
        own_slot(0)
        go(0, 0, 4, to_x_up)
        go(0, 0, 8, to_x_down)
        go(0, 0, 1, to_z_up)
        go(0, 0, 2, to_y_up, cond=even)

    @pl.when(on_b)
    def _():
        own_slot(1)
        go(1, 0, 1, to_x_up)
        go(1, 0, 2, to_x_down)
        go(1, 0, 4, to_z_up)
        go(1, 0, 8, to_y_up, cond=even)

    pltpu.make_async_copy(raw.at[1 - core], raw.at[1 - core], raw_recv).wait()

    @pl.when(on_a)
    def _():
        own_slot(1)

    @pl.when(on_b)
    def _():
        own_slot(0)

    bound = jnp.where(
        (lane128 == GONE)
        | ((lane128 >= BLOCK) & (lane128 < BLOCK + 16) & (lane128 - BLOCK > lax.rem(ctx, 16))),
        -BIG,
        0.0,
    )
    hot = jnp.concatenate(
        [raw[n % 2, (n // 2) * 16 : (n // 2) * 16 + 16, LATENT:] for n in range(8)], 0
    ).astype(jnp.float32)
    bound = jnp.where((lane128 >= DOC) & (lane128 < DOC + 4), (hot - 1.0) * BIG, bound)
    bound = bound.astype(jnp.bfloat16)
    for h in range(HEADS):
        rows = slice(h * TOK, (h + 1) * TOK)
        query[rows, LATENT:] = jnp.where(lane128 < ROPE, query[rows, LATENT:], bound)

    asks, helps = ctx == 16, ctx == 8

    def ask():
        return pltpu.make_async_remote_copy(
            src_ref=hq_out, dst_ref=hq.at[pl.ds(0, TOK + STRIP)],
            send_sem=h_send.at[0], recv_sem=h_recv.at[0], device_id=place(1, zl, x, zh, core),
            device_id_type=MESH,
        )

    def answer():
        return pltpu.make_async_remote_copy(
            src_ref=hout, dst_ref=hin, send_sem=h_send.at[1], recv_sem=h_recv.at[1],
            device_id=place(2, zl, x, zh, core), device_id_type=MESH,
        )

    @pl.when(asks)
    def _():
        for h in range(HEADS):
            hq_out[h * 16 : (h + 1) * 16, :] = query[h * TOK : h * TOK + 16, :]
        part = hq_out[:TOK, LATENT:]
        hq_out[:TOK, LATENT:] = jnp.where(lane128 >= BLOCK, jnp.zeros_like(part), part)
        hq_out[TOK:, :] = keys[0, 0, 0:STRIP, :]
        ask().start()

    both = raw[...].reshape(TOK, WIDE)
    pick = jnp.where(iota((8, 128), 1) == OWNER, 1.0, 0.0).astype(jnp.bfloat16)
    owner = lax.dot_general(pick, both[:, LATENT:], NT, preferred_element_type=jnp.float32)[0:1, :]
    line = iota((64, TOK), 0)
    named = jnp.where(lax.rem(line, 16) < 8, lax.div(line, 16) * 8 + lax.rem(line, 16), -1)
    hits = owner == named.astype(jnp.float32)
    hits_b = jnp.where(hits, 1.0, 0.0).astype(jnp.bfloat16)
    before = nat_of(iota((TOK, TOK), 0)) < nat_of(iota((TOK, TOK), 1))
    rank = lax.dot_general(
        hits_b, jnp.where(before, 1.0, 0.0).astype(jnp.bfloat16), NN,
        preferred_element_type=jnp.float32,
    )
    chosen = jnp.where(hits & (rank == head.astype(jnp.float32)), 1.0, 0.0).astype(jnp.bfloat16)
    rows64 = lax.dot_general(chosen, both, NN, preferred_element_type=jnp.float32)
    counts = lax.dot_general(
        jnp.ones((64, TOK), jnp.bfloat16), both[:, LATENT:], NN, preferred_element_type=jnp.float32
    )
    lane64 = iota((64, 128), 1)
    s1[:, :LATENT] = rows64[:, :LATENT].astype(jnp.bfloat16)
    s1[:, LATENT:] = jnp.where(
        (lane64 >= COUNT) & (lane64 < COUNT + 4), counts, rows64[:, LATENT:]
    ).astype(jnp.bfloat16)
    my_y = pl.ds(pl.multiple_of(y * 16, 16), 16)
    r1[my_y, :] = s1[my_y, :]

    def cache1(d):
        there = lax.rem(y + d, 4)
        return pltpu.make_async_remote_copy(
            src_ref=s1.at[pl.ds(pl.multiple_of(there * 16, 16), 16)], dst_ref=r1.at[my_y],
            send_sem=c1_send.at[d - 1], recv_sem=c1_recv.at[d - 1], device_id=y_peers[d - 1],
            device_id_type=MESH,
        )

    for d in (1, 2, 3):
        cache1(d).start()

    my_group = pl.ds(pl.multiple_of(lane_group * 16, 16), 16)

    def cache2(d):
        there = lax.rem(lane_group + d, 8)
        return pltpu.make_async_remote_copy(
            src_ref=s2.at[pl.ds(pl.multiple_of(there * 16, 16), 16)], dst_ref=r2.at[my_group],
            send_sem=c2_send.at[d - 1], recv_sem=c2_recv.at[d - 1], device_id=group_peers[d - 1],
            device_id_type=MESH,
        )

    def cache_middle():
        for d in (1, 2, 3):
            cache1(d).wait_recv()
        to, source = iota((128, 64), 0), iota((128, 64), 1)
        ys, j = lax.rem(to, 16), lax.div(to, 16)
        permute = jnp.where((ys < 4) & (source == ys * 16 + j), 1.0, 0.0).astype(jnp.bfloat16)
        s2[...] = lax.dot_general(
            permute, r1[...], NN, preferred_element_type=jnp.float32
        ).astype(jnp.bfloat16)
        r2[my_group, :] = s2[my_group, :]
        for d in range(1, 8):
            cache2(d).start()

    def cache_end():
        for d in range(1, 8):
            cache2(d).wait_recv()
        slot, source = iota((32, 128), 0), iota((32, 128), 1)
        permute = jnp.where(
            source == lax.rem(slot, 8) * 16 + lax.div(slot, 8), 1.0, 0.0
        ).astype(jnp.bfloat16)
        rows = lax.dot_general(permute, r2[...], NN, preferred_element_type=jnp.float32)
        facts = rows[:, LATENT:]
        lane32 = iota((32, 128), 1)
        sums = jnp.sum(facts, 0, keepdims=True)
        lane1 = iota((1, 128), 1)

        def lane_of(values, index, at):
            return jnp.sum(jnp.where(at == index, values, 0.0), 1, keepdims=True)

        number = sum(d * lane_of(facts, DOC + d, lane32) for d in (1, 2, 3))
        start = sum(
            jnp.where(number > d, lane_of(sums, COUNT + d, lane1), 0.0) for d in range(3)
        )
        offset = jnp.zeros((32, 1), jnp.float32)
        for d in range(4):
            offset = jnp.where(number == d, off_ref[d].astype(jnp.float32), offset)
        at = (iota((32, 1), 0) * TOK).astype(jnp.float32) + lane_of(facts, NAT, lane32)
        c, s = cos_sin((offset + at - start) * inverse)
        turned = turn(facts, c, sign_sine(s))
        cache_ref[:, :LATENT] = rows[:, :LATENT].astype(jnp.bfloat16)
        cache_ref[:, LATENT:] = turned[:, :ROPE].astype(jnp.bfloat16)

    def a_near():
        @pl.when(on_a)
        def _():
            arrived(0, 1)
            go(0, 1, 5, to_x_up)
            go(0, 1, 9, to_x_down)
            share(0, 1).start()

            @pl.when(odd)
            def _():
                arrived(0, 2)
                go(0, 2, 6, to_x_up, inside=odd)
                go(0, 2, 10, to_x_down, inside=odd)
                go(0, 2, 3, to_z_down, inside=odd)
                share(0, 2).start()
                arrived(0, 3)
                go(0, 3, 7, to_x_up, inside=odd)
                go(0, 3, 11, to_x_down, inside=odd)
                share(0, 3).start()

    def b_near():
        @pl.when(on_b)
        def _():
            arrived(1, 1)
            go(1, 1, 3, to_x_up, half=0)
            go(1, 1, 5, to_z_up)
            go(1, 1, 9, to_y_up, cond=even)
            share(1, 1).start()
            arrived(1, 2)
            go(1, 2, 3, to_x_down, half=1)
            go(1, 2, 6, to_z_down)
            go(1, 2, 10, to_y_up, cond=even)
            share(1, 2).start()
            arrived(1, 3, half=0)
            arrived(1, 3, half=1)
            go(1, 3, 7, to_z_down)
            go(1, 3, 11, to_y_up, cond=even)
            share(1, 3).start()

    def a_far(g):
        def step():
            arrived(0, 4 + g)
            if g in (0, 3):
                go(0, 4 + g, 12 + g, to_x_up, inside=None if g < 2 else odd)
            share(0, 4 + g).start()
            arrived(0, 8 + g)
            if g in (1, 2):
                go(0, 8 + g, 12 + g, to_x_down, inside=None if g < 2 else odd)
            share(0, 8 + g).start()

        pl.when(on_a if g < 2 else on_a & odd)(step)

    def b_far(k):
        @pl.when(on_b & odd)
        def _():
            arrived(1, 8 + k)
            go(1, 8 + k, 12 + k, to_z_up if k < 2 else to_z_down, inside=odd)
            share(1, 8 + k).start()

        @pl.when(on_b)
        def _():
            arrived(1, 4 + k)
            share(1, 4 + k).start()

    def last(k):
        @pl.when(on_a if k < 2 else on_a & odd)
        def _():
            arrived(0, 12 + k)
            share(0, 12 + k).start()

        @pl.when(on_b & odd)
        def _():
            arrived(1, 12 + k)
            share(1, 12 + k).start()

    def shared(chunk):
        for i in range(4):
            slot = chunk * 4 + i
            if slot == 0:
                continue

            @pl.when(on_a if chunk < 2 else on_a & odd)
            def _():
                share(1, slot).wait_recv()

            @pl.when(on_b if i < 2 else on_b & odd)
            def _():
                share(0, slot).wait_recv()

    def scores(chunk, rows, ref):
        q = ref[rows, :]
        out = []
        for scheme in (0, 1):
            k = keys[scheme, chunk * 4 : chunk * 4 + 4].reshape(4 * HALF, WIDE)
            out.append(lax.dot_general(q, k, NT, preferred_element_type=jnp.float32) * SCALE)
        return out

    def absorb(parts, values, rows, first, acc, top, total):
        size = rows.stop - rows.start
        most = jnp.max(functools.reduce(jnp.maximum, parts), 1, keepdims=True)
        if not first:
            old = top[rows, 0:1]
            most = jnp.maximum(old, most)
            shrink = jnp.exp2(old - most)
        weights = [jnp.exp2(p - most) for p in parts]
        added = sum(
            w[:, n * 128 : (n + 1) * 128] for w in weights for n in range(w.shape[1] // 128)
        )
        top[rows, :] = jnp.broadcast_to(most, (size, 128))
        total[rows, :] = added if first else total[rows, :] * shrink + added
        mixed = None
        for w, v in zip(weights, values):
            d = lax.dot_general(w.astype(jnp.bfloat16), v, NN, preferred_element_type=jnp.float32)
            mixed = d if mixed is None else mixed + d
        acc[rows, :] = mixed if first else acc[rows, :] * shrink + mixed

    def latents(chunk):
        return [
            keys[scheme, chunk * 4 : chunk * 4 + 4, :, :LATENT].reshape(4 * HALF, LATENT)
            for scheme in (0, 1)
        ]

    tiles = [slice(i * TILE, (i + 1) * TILE) for i in range(HEADS * TOK // TILE)]

    def tile(chunk, i, parts):
        if chunk == 0:
            masked = []
            for scheme in (0, 1):
                p = parts[scheme]
                own_part = (p[:, :128].reshape(TILE // TOK, TOK, 128) + mask[scheme][None]).reshape(
                    TILE, 128
                )
                masked.append(jnp.concatenate([own_part, p[:, 128:]], 1))
            parts = masked
        absorb(parts, latents(chunk), tiles[i], chunk == 0, acc, top, total)

    all_h = slice(0, TOK)

    def help_first():
        ask().wait_recv()
        strip = hq[TOK:, :]
        p = lax.dot_general(hq[:TOK, :], strip, NT, preferred_element_type=jnp.float32) * SCALE
        p = jnp.where(lane128 <= lax.rem(iota((TOK, 128), 0), 16), p, DEAD)
        absorb([p], [strip[:, :LATENT]], all_h, True, hacc, htop, htotal)

    def help_chunk(chunk):
        absorb(scores(chunk, all_h, hq), latents(chunk), all_h, False, hacc, htop, htotal)

    def help_last():
        hout[...] = (hacc[...] / jnp.sum(htotal[...], 1, keepdims=True)).astype(jnp.bfloat16)
        answer().start()

    a_near()
    b_near()
    shared(0)

    @pl.when(helps)
    def _():
        help_first()
        help_chunk(0)

    parts = scores(0, tiles[0], query)
    for chunk in range(4):
        for i in range(4):
            following = scores(chunk, tiles[i + 1], query) if i < 3 else None
            tile(chunk, i, parts)
            parts = following
            if chunk == 0:
                a_far(i)
                b_far(i)
            if chunk == 1:
                if i == 0:
                    cache_middle()
            if chunk == 2:
                last(i)
        if chunk < 3:
            shared(chunk + 1)

            @pl.when(helps)
            def _():
                help_chunk(chunk + 1)
                if chunk == 2:
                    help_last()

            parts = scores(chunk + 1, tiles[0], query)
        if chunk == 2:
            cache_end()

    @pl.when(asks)
    def _():
        answer().wait_recv()

    locals_[5].wait()
    spare = iota((TOK, LATENT), 0) < 8
    for h in range(HEADS):
        rows = slice(h * TOK, (h + 1) * TOK)
        latent = (acc[rows, :] / jnp.sum(total[rows, :], 1, keepdims=True)).astype(jnp.bfloat16)
        theirs = jnp.concatenate(
            [hin[h * 16 : (h + 1) * 16, :], jnp.zeros((TOK - 16, LATENT), jnp.bfloat16)], 0
        )
        latent = jnp.where(spare & asks, theirs, latent)
        out_ref[:, h * VDIM : (h + 1) * VDIM] = lax.dot_general(
            latent, wv[h], NN, preferred_element_type=jnp.float32
        ).astype(jnp.bfloat16)

    for copy in pa:
        copy.wait_send()
    share_raw.wait_send()
    for scheme, on in ((0, on_a), (1, on_b)):
        @pl.when(on)
        def _():
            for make, cond in plan[scheme]:
                if cond is None:
                    make().wait_send()
                else:
                    @pl.when(cond)
                    def _():
                        make().wait_send()
            for slot in range(1, 16):
                g = slot % 4 if scheme == 0 else slot // 4
                if g < 2:
                    share(scheme, slot).wait_send()
                else:
                    @pl.when(odd)
                    def _():
                        share(scheme, slot).wait_send()
    for d in (1, 2, 3):
        cache1(d).wait_send()
    for d in range(1, 8):
        cache2(d).wait_send()

    @pl.when(asks)
    def _():
        ask().wait_send()

    @pl.when(helps)
    def _():
        answer().wait_send()


def local(q_nope, q_rope, key_latent, doc_ids, doc_offsets, owners, w_key, w_value):
    bf, f32 = jnp.bfloat16, jnp.float32
    vmem = pltpu.VMEM
    dma = pltpu.SemaphoreType.DMA
    hbm = pl.BlockSpec(memory_space=pl.ANY)
    smem = pl.BlockSpec(memory_space=pltpu.SMEM)
    rows = HEADS * TOK
    return pl.pallas_call(
        kernel,
        out_shape=(
            jax.ShapeDtypeStruct((TOK, HEADS * VDIM), bf),
            jax.ShapeDtypeStruct((32, LATENT + ROPE), bf),
        ),
        in_specs=[hbm, hbm, hbm, smem, smem, hbm, hbm, hbm],
        out_specs=(pl.BlockSpec(memory_space=vmem), pl.BlockSpec(memory_space=vmem)),
        scratch_shapes=[
            vmem((TOK, HEADS * NOPE), bf),
            vmem((TOK, HEADS * ROPE), bf),
            vmem((STRIP, LATENT + ROPE), bf),
            vmem((STRIP, 1), jnp.int32),
            vmem((HEADS, NOPE, LATENT), bf),
            vmem((HEADS, LATENT, VDIM), bf),
            vmem((2, HALF, WIDE), bf),
            vmem((2, 16, HALF, WIDE), bf),
            vmem((rows, WIDE), bf),
            vmem((rows, LATENT), f32),
            vmem((rows, 128), f32),
            vmem((rows, 128), f32),
            vmem((2, TOK, 128), f32),
            vmem((TOK, 128), f32),
            vmem((TOK, 128), f32),
            vmem((64, WIDE), bf),
            vmem((64, WIDE), bf),
            vmem((128, WIDE), bf),
            vmem((128, WIDE), bf),
            vmem((TOK + STRIP, WIDE), bf),
            vmem((2 * TOK, WIDE), bf),
            vmem((TOK, LATENT), f32),
            vmem((TOK, 128), f32),
            vmem((TOK, 128), f32),
            vmem((TOK, LATENT), bf),
            vmem((TOK, LATENT), bf),
            dma((6,)),
            dma((3,)),
            dma((3,)),
            dma,
            dma,
            dma((24,)),
            dma((17,)),
            dma((16,)),
            dma((16,)),
            dma((3,)),
            dma((3,)),
            dma((7,)),
            dma((7,)),
            dma((2,)),
            dma((2,)),
        ],
        compiler_params=pltpu.CompilerParams(
            collective_id=0, has_side_effects=True, vmem_limit_bytes=48 * 2**20
        ),
        name="latent_attention",
    )(q_nope, q_rope, key_latent, doc_ids, doc_offsets, owners, w_key, w_value)


def solution(mesh):
    in_specs = (
        P("ctx", "head"),
        P("ctx", "head"),
        P(("ctx", "head"), None),
        P(("ctx", "head")),
        P(),
        P(("ctx", "head"), None),
        P("head", None, None),
        P("head", None, None),
    )
    out_specs = (P("ctx", "head"), P(("ctx", "head"), None))
    return jax.shard_map(local, mesh=mesh, in_specs=in_specs, out_specs=out_specs, check_vma=False)
```

```python
import functools

import jax
import jax.numpy as jnp
import numpy as np
from jax import lax
from jax.experimental import pallas as pl
from jax.experimental.pallas import tpu as pltpu
from jax.sharding import PartitionSpec as P

NOPE = 128
ROPE = 64
LATENT = 512
VDIM = 128
HEADS = 8
TOK = 128
HALF = 64
WIDE = 640
STRIP = 16
TILE = 256
BIG = float(2.0**100)
DEAD = -1e30
SCALE = (NOPE + ROPE) ** -0.5 * 1.4426950408889634
INVERSE = [float(v) for v in (10000.0 ** (-2.0 * np.arange(32) / 64.0)).astype(np.float32)]
DOC = 64
GONE = 68
NAT = 69
OWNER = 70
COUNT = 72
BLOCK = 80
EXTRA = 64

ORDER = (
    (0, 0), (0, 1), (1, 0), (2, 0), (0, 2), (0, 3), (3, 0), (1, 1),
    (2, 1), (3, 1), (1, 2), (2, 2), (3, 2), (1, 3), (2, 3), (3, 3),
)
CHUNKS = ((0, 2), (2, 6), (6, 10), (10, 14), (14, 16))

MESH = pl.DeviceIdType.MESH
NT = (((1,), (1,)), ((), ()))
NN = (((1,), (0,)), ((), ()))


def iota(shape, dim):
    return lax.broadcasted_iota(jnp.int32, shape, dim)


def place(y, zl, x, zh, core):
    return (lax.rem(y, 4) * 8 + lax.rem(zl, 2) * 4 + lax.rem(x, 4), lax.rem(zh, 4) * 2 + core)


def inverse_lanes(shape):
    index = lax.rem(iota(shape, 1), 32)
    out = jnp.zeros(shape, jnp.float32)
    for j, value in enumerate(INVERSE):
        out = jnp.where(index == j, value, out)
    return out


def cos_sin(angle):
    turns = jnp.floor(angle * 0.6366197723675814 + 0.5)
    rest = angle - turns * 1.5703125
    rest = rest - turns * 4.837512969970703125e-4
    rest = rest - turns * 7.54978995489188216e-8
    z = rest * rest
    sine = rest + rest * z * (
        -1.6666654611e-1 + z * (8.3321608736e-3 - z * 1.9515295891e-4)
    )
    cosine = 1.0 - 0.5 * z + z * z * (
        4.166664568298827e-2 + z * (-1.388731625493765e-3 + z * 2.443315711809948e-5)
    )
    quadrant = turns.astype(jnp.int32) & 3
    swap = (quadrant & 1) == 1
    c = jnp.where(swap, sine, cosine)
    s = jnp.where(swap, cosine, sine)
    c = jnp.where((quadrant == 1) | (quadrant == 2), -c, c)
    s = jnp.where(quadrant >= 2, -s, s)
    return c, s


def turn(values, cosine, signed_sine):
    first = lax.rem(iota(values.shape, 1), 64) < 32
    partner = jnp.where(first, pltpu.roll(values, 96, 1), pltpu.roll(values, 32, 1))
    return values * cosine + partner * signed_sine


def sign_sine(sine):
    return jnp.where(lax.rem(iota(sine.shape, 1), 64) < 32, -sine, sine)


def nat_of(k):
    return lax.div(lax.rem(k, 64), 16) * 32 + lax.div(k, 64) * 16 + lax.rem(k, 16)


def kernel(
    qn_hbm, qr_hbm, kl_hbm, doc_ref, off_ref, own_ref, wk_hbm, wv_hbm,
    out_hbm, cache_ref,
    qn, qr, kl, wk, wv, raw, keys, query, acc, top, total, mask, cos_t, sin_t, cos_p, sin_p, raw_p,
    s1, r1, s2, r2, strip, hq_out, hout, hin, out_v,
    local_sem, pa_send, pa_recv, raw_send, raw_recv, m_send, m_recv, sib_send, sib_recv,
    c1_send, c1_recv, c2_send, c2_recv, h_send, h_recv,
):
    ctx = lax.axis_index("ctx")
    head = lax.axis_index("head")
    y, zl, x = lax.div(ctx, 8), lax.rem(lax.div(ctx, 4), 2), lax.rem(ctx, 4)
    zh, core = lax.div(head, 2), lax.rem(head, 2)
    odd = lax.rem(y, 2) == 1
    even = lax.rem(y, 2) == 0
    lane_group = zl * 4 + x

    z_up = lax.rem(zh * 2 + zl + 1, 8)
    z_down = lax.rem(zh * 2 + zl + 7, 8)
    to_z_up = place(y, lax.rem(z_up, 2), x, lax.div(z_up, 2), core)
    to_z_down = place(y, lax.rem(z_down, 2), x, lax.div(z_down, 2), core)
    to_x_up = place(y, zl, x + 1, zh, core)
    to_x_down = place(y, zl, x + 3, zh, core)
    to_x_across = place(y, zl, x + 2, zh, core)
    to_y_up = place(y + 1, zl, x, zh, core)
    sibling = (ctx, zh * 2 + 1 - core)
    z_peers = []
    for d in range(1, 8):
        z = lax.rem(zh * 2 + zl + d, 8)
        z_peers.append(place(y, lax.rem(z, 2), x, lax.div(z, 2), core))
    y_peers = [place(y + d, zl, x, zh, core) for d in (1, 2, 3)]
    group_peers = []
    for d in range(1, 8):
        j = lax.rem(lane_group + d, 8)
        group_peers.append(place(y, lax.div(j, 4), lax.rem(j, 4), zh, core))
    barrier = pltpu.get_barrier_semaphore()
    greeted = z_peers + y_peers + group_peers[:3] + group_peers[4:] + [sibling]
    for peer in greeted:
        pl.semaphore_signal(barrier, inc=1, device_id=peer, device_id_type=MESH)

    locals_ = [
        pltpu.make_async_copy(kl_hbm, kl, local_sem.at[0]),
        pltpu.make_async_copy(qr_hbm, qr, local_sem.at[1]),
        pltpu.make_async_copy(qn_hbm, qn, local_sem.at[2]),
        pltpu.make_async_copy(wk_hbm, wk, local_sem.at[3]),
        pltpu.make_async_copy(wv_hbm, wv, local_sem.at[4]),
    ]
    for copy in locals_:
        copy.start()
    lane128 = iota((TOK, 128), 1)

    @pl.when(even)
    def _():
        blank = jnp.where(iota((HALF, 128), 1) == GONE, 1.0, 0.0).astype(jnp.bfloat16)
        zero = jnp.zeros((HALF, LATENT), jnp.bfloat16)
        for scheme in (0, 1):
            for pos, (_, g) in enumerate(ORDER):
                if g >= 2:
                    keys[pos, scheme, :, :LATENT] = zero
                    keys[pos, scheme, :, LATENT:] = blank

    @pl.when(ctx != 8)
    def _():
        query[HEADS * TOK :, :] = jnp.zeros((EXTRA, WIDE), jnp.bfloat16)

    top[HEADS * TOK :, :] = jnp.zeros((EXTRA, 128), jnp.float32)
    total[HEADS * TOK :, :] = jnp.zeros((EXTRA, 128), jnp.float32)
    acc[HEADS * TOK :, :] = jnp.zeros((EXTRA, LATENT), jnp.float32)
    rest = TOK - STRIP
    strip[STRIP:, :LATENT] = jnp.zeros((rest, LATENT), jnp.bfloat16)
    strip[STRIP:, LATENT:] = jnp.where(iota((rest, 128), 1) == GONE, 1.0, 0.0).astype(jnp.bfloat16)
    inverse = inverse_lanes((8, 128))[0:1, :]
    token = (ctx * TOK + iota((TOK, 128), 0)).astype(jnp.float32)
    c, s = cos_sin(token * inverse)
    cos_t[...] = c
    sin_t[...] = sign_sine(s)
    other = y * 8 + (1 - zl) * 4 + x
    k = iota((HALF, 128), 0)
    at = other * TOK + lax.div(k, 16) * 32 + core * 16 + lax.rem(k, 16)
    c, s = cos_sin(at.astype(jnp.float32) * inverse)
    cos_p[...] = c
    sin_p[...] = sign_sine(s)
    mask[...] = jnp.where(nat_of(lane128) > iota((TOK, 128), 0), DEAD, 0.0)

    docs = jnp.zeros((STRIP, 128), jnp.int32)
    owners = docs
    for r in range(STRIP):
        docs = jnp.where(iota((STRIP, 128), 0) == r, doc_ref[r], docs)
        owners = jnp.where(iota((STRIP, 128), 0) == r, own_ref[r], owners)
    lane = iota((STRIP, 128), 1)
    locals_[0].wait()
    facts = jnp.where((lane == DOC + docs) | (lane == COUNT + docs), 1.0, 0.0)
    facts = jnp.where(lane == BLOCK + lax.rem(ctx, 16), 1.0, facts)
    facts = jnp.where(lane == NAT, (head * STRIP + iota((STRIP, 128), 0)).astype(jnp.float32), facts)
    facts = jnp.where(lane == OWNER, owners.astype(jnp.float32), facts)
    mine = pl.ds(pl.multiple_of(zh * STRIP, STRIP), STRIP)
    raw[core, mine, :LATENT] = kl[:, :LATENT]
    raw[core, mine, LATENT:] = jnp.concatenate(
        [kl[:, LATENT:], facts[:, ROPE:].astype(jnp.bfloat16)], 1
    )
    pl.semaphore_wait(barrier, len(greeted))

    pa = [
        pltpu.make_async_remote_copy(
            src_ref=raw.at[core, mine],
            dst_ref=raw.at[core, mine] if d % 2 == 0 else raw_p.at[mine],
            send_sem=pa_send.at[d - 1], recv_sem=pa_recv.at[d - 1],
            device_id=z_peers[d - 1], device_id_type=MESH,
        )
        for d in range(1, 8)
    ]
    for d in (4, 2, 6, 3, 5, 1, 7):
        pa[d - 1].start()

    locals_[1].wait()
    for pair in range(4):
        v = turn(qr[:, pair * 128 : pair * 128 + 128].astype(jnp.float32), cos_t[...], sin_t[...])
        base = pair * 2 * TOK
        query[base : base + TOK, LATENT:] = v.astype(jnp.bfloat16)
        query[base + TOK : base + 2 * TOK, LATENT:] = pltpu.roll(v, 64, 1).astype(jnp.bfloat16)
    locals_[2].wait()
    locals_[3].wait()
    for h in range(HEADS):
        a = lax.dot_general(
            qn[:, h * NOPE : (h + 1) * NOPE], wk[h], NN, preferred_element_type=jnp.float32
        )
        query[h * TOK : (h + 1) * TOK, :LATENT] = a.astype(jnp.bfloat16)

    plan = {0: {}, 1: {}}

    def send(scheme, src, dst, to, sem):
        return pltpu.make_async_remote_copy(
            src_ref=keys.at[src, scheme], dst_ref=keys.at[dst, scheme],
            send_sem=m_send.at[sem], recv_sem=m_recv.at[dst], device_id=to, device_id_type=MESH,
        )

    def go(scheme, src, dst, to, cond=None, inside=None):
        src, dst = ORDER.index(src), ORDER.index(dst)
        make = functools.partial(send, scheme, src, dst, to, len(plan[scheme]))
        plan[scheme][src, dst, cond is None] = (make, cond if inside is None else inside)
        if cond is None:
            make().start()
        else:
            @pl.when(cond)
            def _():
                make().start()

    def arrived(scheme, pos):
        ref = keys.at[pos, scheme]
        pltpu.make_async_copy(ref, ref, m_recv.at[pos]).wait()

    def share(scheme, pos):
        return pltpu.make_async_remote_copy(
            src_ref=keys.at[pos, scheme], dst_ref=keys.at[pos, scheme],
            send_sem=sib_send.at[pos], recv_sem=sib_recv.at[pos],
            device_id=sibling, device_id_type=MESH,
        )

    def fill(scheme, pos, rows, cc, ss):
        v = rows[:, LATENT:].astype(jnp.float32)
        rotated = jnp.where(iota((HALF, 128), 1) < ROPE, turn(v, cc, ss), v)
        keys[pos, scheme, :, :LATENT] = rows[:, :LATENT]
        keys[pos, scheme, :, LATENT:] = rotated.astype(jnp.bfloat16)

    def own_slot(half):
        cc = jnp.concatenate([cos_t[n * 32 + half * 16 : n * 32 + half * 16 + 16, :] for n in range(4)], 0)
        ss = jnp.concatenate([sin_t[n * 32 + half * 16 : n * 32 + half * 16 + 16, :] for n in range(4)], 0)
        fill(half, 0, raw[half], cc, ss)

    for d in (2, 4, 6):
        pa[d - 1].wait_recv()
    share_raw = pltpu.make_async_remote_copy(
        src_ref=raw.at[core], dst_ref=raw.at[core], send_sem=raw_send, recv_sem=raw_recv,
        device_id=sibling, device_id_type=MESH,
    )
    share_raw.start()

    on_a, on_b = core == 0, core == 1

    @pl.when(on_a)
    def _():
        own_slot(0)
        go(0, (0, 0), (0, 2), to_y_up, cond=even)

    @pl.when(on_b)
    def _():
        own_slot(1)
        go(1, (0, 0), (1, 0), to_x_up)
        go(1, (0, 0), (2, 0), to_x_down)
        go(1, (0, 0), (3, 0), to_x_across)

    for d in (1, 3, 5, 7):
        pa[d - 1].wait_recv()

    @pl.when(on_a)
    def _():
        fill(0, 1, raw_p[...], cos_p[...], sin_p[...])
        go(0, (0, 1), (0, 3), to_y_up, cond=even)
        go(0, (0, 0), (1, 0), to_x_up)
        go(0, (0, 0), (2, 0), to_x_down)
        go(0, (0, 0), (3, 0), to_x_across)
        share(0, 1).start()

    @pl.when(on_b)
    def _():
        fill(1, 1, raw_p[...], cos_p[...], sin_p[...])
        go(1, (0, 0), (0, 2), to_y_up, cond=even)
        go(1, (0, 1), (0, 3), to_y_up, cond=even)
        share(1, 1).start()

    pltpu.make_async_copy(raw.at[1 - core], raw.at[1 - core], raw_recv).wait()

    @pl.when(on_a)
    def _():
        own_slot(1)

    @pl.when(on_b)
    def _():
        own_slot(0)

    bound = jnp.where(
        (lane128 == GONE)
        | ((lane128 >= BLOCK) & (lane128 < BLOCK + 16) & (lane128 - BLOCK > lax.rem(ctx, 16))),
        -BIG,
        0.0,
    )
    hot = jnp.concatenate(
        [raw[n % 2, (n // 2) * 16 : (n // 2) * 16 + 16, LATENT:] for n in range(8)], 0
    ).astype(jnp.float32)
    bound = jnp.where((lane128 >= DOC) & (lane128 < DOC + 4), (hot - 1.0) * BIG, bound)
    bound = bound.astype(jnp.bfloat16)
    for h in range(HEADS):
        rows = slice(h * TOK, (h + 1) * TOK)
        query[rows, LATENT:] = jnp.where(lane128 < ROPE, query[rows, LATENT:], bound)

    asks, helps = ctx == 16, ctx == 8

    extra = slice(HEADS * TOK, HEADS * TOK + EXTRA)

    def ask(part):
        return pltpu.make_async_remote_copy(
            src_ref=hq_out.at[pl.ds(0, EXTRA) if part == 0 else pl.ds(EXTRA, STRIP)],
            dst_ref=query.at[pl.ds(HEADS * TOK, EXTRA)] if part == 0 else strip.at[pl.ds(0, STRIP)],
            send_sem=h_send.at[part], recv_sem=h_recv.at[part],
            device_id=place(1, zl, x, zh, core), device_id_type=MESH,
        )

    def answer():
        return pltpu.make_async_remote_copy(
            src_ref=hout, dst_ref=hin, send_sem=h_send.at[2], recv_sem=h_recv.at[2],
            device_id=place(2, zl, x, zh, core), device_id_type=MESH,
        )

    @pl.when(asks)
    def _():
        firsts = jnp.concatenate(
            [query[h * TOK : h * TOK + 16, :].astype(jnp.float32)[:8] for h in range(HEADS)], 0
        )
        firsts = jnp.where(iota((EXTRA, WIDE), 1) >= LATENT + BLOCK, 0.0, firsts)
        hq_out[:EXTRA, :] = firsts.astype(jnp.bfloat16)
        hq_out[EXTRA:, :] = keys[0, 0, 0:STRIP, :]
        ask(0).start()
        ask(1).start()

    my_y = pl.ds(pl.multiple_of(y * 16, 16), 16)

    def cache1(d):
        there = lax.rem(y + d, 4)
        return pltpu.make_async_remote_copy(
            src_ref=s1.at[pl.ds(pl.multiple_of(there * 16, 16), 16)], dst_ref=r1.at[my_y],
            send_sem=c1_send.at[d - 1], recv_sem=c1_recv.at[d - 1], device_id=y_peers[d - 1],
            device_id_type=MESH,
        )

    def cache_begin():
        both = raw[...].reshape(TOK, WIDE)
        pick = jnp.where(iota((8, 128), 1) == OWNER, 1.0, 0.0).astype(jnp.bfloat16)
        owner = lax.dot_general(pick, both[:, LATENT:], NT, preferred_element_type=jnp.float32)[0:1, :]
        line = iota((64, TOK), 0)
        named = jnp.where(lax.rem(line, 16) < 8, lax.div(line, 16) * 8 + lax.rem(line, 16), -1)
        hits = owner == named.astype(jnp.float32)
        hits_b = jnp.where(hits, 1.0, 0.0).astype(jnp.bfloat16)
        before = nat_of(iota((TOK, TOK), 0)) < nat_of(iota((TOK, TOK), 1))
        rank = lax.dot_general(
            hits_b, jnp.where(before, 1.0, 0.0).astype(jnp.bfloat16), NN,
            preferred_element_type=jnp.float32,
        )
        chosen = jnp.where(hits & (rank == head.astype(jnp.float32)), 1.0, 0.0).astype(jnp.bfloat16)
        rows64 = lax.dot_general(chosen, both, NN, preferred_element_type=jnp.float32)
        counts = lax.dot_general(
            jnp.ones((64, TOK), jnp.bfloat16), both[:, LATENT:], NN, preferred_element_type=jnp.float32
        )
        lane64 = iota((64, 128), 1)
        s1[:, :LATENT] = rows64[:, :LATENT].astype(jnp.bfloat16)
        s1[:, LATENT:] = jnp.where(
            (lane64 >= COUNT) & (lane64 < COUNT + 4), counts, rows64[:, LATENT:]
        ).astype(jnp.bfloat16)
        r1[my_y, :] = s1[my_y, :]
        for d in (1, 2, 3):
            cache1(d).start()

    my_group = pl.ds(pl.multiple_of(lane_group * 16, 16), 16)

    def cache2(d):
        there = lax.rem(lane_group + d, 8)
        return pltpu.make_async_remote_copy(
            src_ref=s2.at[pl.ds(pl.multiple_of(there * 16, 16), 16)], dst_ref=r2.at[my_group],
            send_sem=c2_send.at[d - 1], recv_sem=c2_recv.at[d - 1], device_id=group_peers[d - 1],
            device_id_type=MESH,
        )

    def cache_middle():
        for d in (1, 2, 3):
            cache1(d).wait_recv()
        to, source = iota((128, 64), 0), iota((128, 64), 1)
        ys, j = lax.rem(to, 16), lax.div(to, 16)
        permute = jnp.where((ys < 4) & (source == ys * 16 + j), 1.0, 0.0).astype(jnp.bfloat16)
        s2[...] = lax.dot_general(
            permute, r1[...], NN, preferred_element_type=jnp.float32
        ).astype(jnp.bfloat16)
        r2[my_group, :] = s2[my_group, :]
        for d in range(1, 8):
            cache2(d).start()

    def cache_end():
        for d in range(1, 8):
            cache2(d).wait_recv()
        slot, source = iota((32, 128), 0), iota((32, 128), 1)
        permute = jnp.where(
            source == lax.rem(slot, 8) * 16 + lax.div(slot, 8), 1.0, 0.0
        ).astype(jnp.bfloat16)
        rows = lax.dot_general(permute, r2[...], NN, preferred_element_type=jnp.float32)
        facts = rows[:, LATENT:]
        lane32 = iota((32, 128), 1)
        sums = jnp.sum(facts, 0, keepdims=True)
        lane1 = iota((1, 128), 1)

        def lane_of(values, index, at):
            return jnp.sum(jnp.where(at == index, values, 0.0), 1, keepdims=True)

        number = sum(d * lane_of(facts, DOC + d, lane32) for d in (1, 2, 3))
        start = sum(
            jnp.where(number > d, lane_of(sums, COUNT + d, lane1), 0.0) for d in range(3)
        )
        offset = jnp.zeros((32, 1), jnp.float32)
        for d in range(4):
            offset = jnp.where(number == d, off_ref[d].astype(jnp.float32), offset)
        at = (iota((32, 1), 0) * TOK).astype(jnp.float32) + lane_of(facts, NAT, lane32)
        c, s = cos_sin((offset + at - start) * inverse)
        turned = turn(facts, c, sign_sine(s))
        cache_ref[:, :LATENT] = rows[:, :LATENT].astype(jnp.bfloat16)
        cache_ref[:, LATENT:] = turned.astype(jnp.bfloat16)

    def step(pos):
        xr, g = here = ORDER[pos]
        inside = None if g < 2 else odd

        @pl.when(on_a if g < 2 else on_a & odd)
        def _():
            arrived(0, pos)
            if xr == 0:
                go(0, here, (1, g), to_x_up, inside=inside)
                go(0, here, (2, g), to_x_down, inside=inside)
                go(0, here, (3, g), to_x_across, inside=inside)
            if g == 0:
                go(0, here, (xr, 1), to_z_up if xr == 1 else to_z_down)
            share(0, pos).start()

        @pl.when(on_b if g < 2 else on_b & odd)
        def _():
            arrived(1, pos)
            if g == 0:
                go(1, here, (xr, 2), to_y_up, cond=even)
                go(1, here, (xr, 1), to_z_down if xr == 2 else to_z_up)
            if g == 2 and xr > 0:
                go(1, here, (xr, 3), to_z_up if xr == 1 else to_z_down, inside=odd)
            share(1, pos).start()

    def shared(chunk):
        for pos in range(*CHUNKS[chunk]):
            if pos == 0:
                continue

            @pl.when(on_a if ORDER[pos][1] < 2 else on_a & odd)
            def _():
                share(1, pos).wait_recv()

            @pl.when(on_b if ORDER[pos][1] < 2 else on_b & odd)
            def _():
                share(0, pos).wait_recv()

    def rows_of(chunk):
        first, end = CHUNKS[chunk]
        return keys[first:end].reshape((end - first) * TOK, WIDE)

    def scores(q, k):
        return lax.dot_general(q, k, NT, preferred_element_type=jnp.float32) * SCALE

    def absorb(p, values, rows, first):
        size = rows.stop - rows.start
        most = jnp.max(p, 1, keepdims=True)
        if not first:
            old = top[rows, 0:1]
            most = jnp.maximum(old, most)
            shrink = jnp.exp2(old - most)
        weights = jnp.exp2(p - most)
        added = sum(weights[:, n * 128 : (n + 1) * 128] for n in range(p.shape[1] // 128))
        top[rows, :] = jnp.broadcast_to(most, (size, 128))
        total[rows, :] = added if first else total[rows, :] * shrink + added
        mixed = lax.dot_general(
            weights.astype(jnp.bfloat16), values, NN, preferred_element_type=jnp.float32
        )
        acc[rows, :] = mixed if first else acc[rows, :] * shrink + mixed

    count = HEADS * TOK // TILE
    tiles = [slice(i * TILE, (i + 1) * TILE) for i in range(count)]
    wide_tiles = tiles[:-1] + [slice(tiles[-1].start, extra.stop)]

    def tile(chunk, rows, p):
        if chunk == 0:
            own_part = p[:, :TOK].reshape(TILE // TOK, TOK, TOK) + mask[...][None]
            p = jnp.concatenate([own_part.reshape(TILE, TOK), p[:, TOK:]], 1)
        absorb(p, rows_of(chunk)[:, :LATENT], rows, chunk == 0)

    def sweep(chunk, order, after_first=None):
        p = scores(query[order[0], :], rows_of(chunk))
        for i, rows in enumerate(order):
            following = None
            if i + 1 < len(order):
                following = scores(query[order[i + 1], :], rows_of(chunk))
            tile(chunk, rows, p)
            p = following
            if i == 0 and after_first is not None:
                after_first()

    def help_first():
        ask(0).wait_recv()
        ask(1).wait_recv()
        p = scores(query[extra, :], strip[...])
        p = jnp.where(iota((EXTRA, TOK), 1) <= lax.rem(iota((EXTRA, TOK), 0), 8), p, DEAD)
        absorb(p, strip[:, :LATENT], extra, True)
        absorb(scores(query[extra, :], rows_of(0)), rows_of(0)[:, :LATENT], extra, False)

    def help_last():
        hout[...] = (acc[extra, :] / jnp.sum(total[extra, :], 1, keepdims=True)).astype(
            jnp.bfloat16
        )
        answer().start()

    cache_begin()
    shared(0)
    sweep(0, tiles)
    for pos in range(2, 6):
        step(pos)

    @pl.when(helps)
    def _():
        help_first()

    cache_middle()
    shared(1)
    sweep(1, wide_tiles)
    for pos in range(6, 13):
        step(pos)
    shared(2)

    @pl.when(helps)
    def _():
        sweep(2, [extra])

    @pl.when(jnp.logical_not(helps))
    def _():
        sweep(2, tiles)

    step(13)
    shared(3)
    sweep(3, wide_tiles)
    step(14)
    step(15)
    cache_end()
    shared(4)
    sweep(4, wide_tiles[::-1], lambda: pl.when(helps)(help_last))

    @pl.when(asks)
    def _():
        answer().wait_recv()
        theirs = hin[...].astype(jnp.float32)
        for h in range(HEADS):
            rows = slice(h * TOK, h * TOK + 8)
            acc[rows, :] = theirs[h * 8 : (h + 1) * 8]
            total[rows, :] = jnp.where(iota((8, 128), 1) == 0, 1.0, 0.0)

    locals_[4].wait()

    def store(part):
        columns = pl.ds(part * 4 * VDIM, 4 * VDIM)
        return pltpu.make_async_copy(
            out_v.at[:, columns], out_hbm.at[:, columns], local_sem.at[part]
        )

    for h in range(HEADS):
        rows = slice(h * TOK, (h + 1) * TOK)
        share_of = 1.0 / jnp.sum(total[rows, :], 1, keepdims=True)
        latent = (acc[rows, :] * share_of).astype(jnp.bfloat16)
        out_v[:, h * VDIM : (h + 1) * VDIM] = lax.dot_general(
            latent, wv[h], NN, preferred_element_type=jnp.float32
        ).astype(jnp.bfloat16)
        if h % 4 == 3:
            store(h // 4).start()

    store(0).wait()
    store(1).wait()
    for copy in pa:
        copy.wait_send()
    share_raw.wait_send()
    for scheme, on in ((0, on_a), (1, on_b)):
        @pl.when(on)
        def _():
            for make, cond in plan[scheme].values():
                if cond is None:
                    make().wait_send()
                else:
                    @pl.when(cond)
                    def _():
                        make().wait_send()
            for pos in range(1, 16):
                if ORDER[pos][1] < 2:
                    share(scheme, pos).wait_send()
                else:
                    @pl.when(odd)
                    def _():
                        share(scheme, pos).wait_send()
    for d in (1, 2, 3):
        cache1(d).wait_send()
    for d in range(1, 8):
        cache2(d).wait_send()

    @pl.when(asks)
    def _():
        ask(0).wait_send()
        ask(1).wait_send()

    @pl.when(helps)
    def _():
        answer().wait_send()


def local(q_nope, q_rope, key_latent, doc_ids, doc_offsets, owners, w_key, w_value):
    bf, f32 = jnp.bfloat16, jnp.float32
    vmem = pltpu.VMEM
    dma = pltpu.SemaphoreType.DMA
    hbm = pl.BlockSpec(memory_space=pl.ANY)
    smem = pl.BlockSpec(memory_space=pltpu.SMEM)
    rows = HEADS * TOK
    attended, cache = pl.pallas_call(
        kernel,
        out_shape=(
            jax.ShapeDtypeStruct((TOK, HEADS * VDIM), bf),
            jax.ShapeDtypeStruct((32, WIDE), bf),
        ),
        in_specs=[hbm, hbm, hbm, smem, smem, smem, hbm, hbm],
        out_specs=(hbm, pl.BlockSpec(memory_space=vmem)),
        scratch_shapes=[
            vmem((TOK, HEADS * NOPE), bf),
            vmem((TOK, HEADS * ROPE), bf),
            vmem((STRIP, LATENT + ROPE), bf),
            vmem((HEADS, NOPE, LATENT), bf),
            vmem((HEADS, LATENT, VDIM), bf),
            vmem((2, HALF, WIDE), bf),
            vmem((16, 2, HALF, WIDE), bf),
            vmem((rows + EXTRA, WIDE), bf),
            vmem((rows + EXTRA, LATENT), f32),
            vmem((rows + EXTRA, 128), f32),
            vmem((rows + EXTRA, 128), f32),
            vmem((TOK, 128), f32),
            vmem((TOK, 128), f32),
            vmem((TOK, 128), f32),
            vmem((HALF, 128), f32),
            vmem((HALF, 128), f32),
            vmem((HALF, WIDE), bf),
            vmem((64, WIDE), bf),
            vmem((64, WIDE), bf),
            vmem((128, WIDE), bf),
            vmem((128, WIDE), bf),
            vmem((TOK, WIDE), bf),
            vmem((EXTRA + STRIP, WIDE), bf),
            vmem((EXTRA, LATENT), bf),
            vmem((EXTRA, LATENT), bf),
            vmem((TOK, HEADS * VDIM), bf),
            dma((5,)),
            dma((7,)),
            dma((7,)),
            dma,
            dma,
            dma((24,)),
            dma((16,)),
            dma((16,)),
            dma((16,)),
            dma((3,)),
            dma((3,)),
            dma((7,)),
            dma((7,)),
            dma((3,)),
            dma((3,)),
        ],
        compiler_params=pltpu.CompilerParams(
            collective_id=0, has_side_effects=True, vmem_limit_bytes=60 * 2**20
        ),
        name="latent_attention",
    )(q_nope, q_rope, key_latent, doc_ids, doc_offsets, owners.reshape(STRIP), w_key, w_value)
    return attended, cache[:, : LATENT + ROPE]


def solution(mesh):
    in_specs = (
        P("ctx", "head"),
        P("ctx", "head"),
        P(("ctx", "head"), None),
        P(("ctx", "head")),
        P(),
        P(("ctx", "head"), None),
        P("head", None, None),
        P("head", None, None),
    )
    out_specs = (P("ctx", "head"), P(("ctx", "head"), None))
    return jax.shard_map(local, mesh=mesh, in_specs=in_specs, out_specs=out_specs, check_vma=False)
```

```python
import functools

import jax
import jax.numpy as jnp
import numpy as np
from jax import lax
from jax.experimental import pallas as pl
from jax.experimental.pallas import tpu as pltpu
from jax.sharding import PartitionSpec as P

NOPE = 128
ROPE = 64
LATENT = 512
VDIM = 128
HEADS = 8
TOK = 128
HALF = 64
WIDE = 640
STRIP = 16
TILE = 256
BIG = float(2.0**100)
DEAD = -1e30
SCALE = (NOPE + ROPE) ** -0.5 * 1.4426950408889634
INVERSE = [float(v) for v in (10000.0 ** (-2.0 * np.arange(32) / 64.0)).astype(np.float32)]
DOC = 64
GONE = 68
NAT = 69
OWNER = 70
COUNT = 72
BLOCK = 80
EXTRA = 64

ORDER = (
    (0, 0), (0, 1), (1, 0), (2, 0), (0, 2), (0, 3), (3, 0), (1, 1),
    (2, 1), (3, 1), (1, 2), (2, 2), (3, 2), (1, 3), (2, 3), (3, 3),
)
CHUNKS = ((0, 2), (2, 6), (6, 10), (10, 14), (14, 16))

MESH = pl.DeviceIdType.MESH
NT = (((1,), (1,)), ((), ()))
NN = (((1,), (0,)), ((), ()))


def iota(shape, dim):
    return lax.broadcasted_iota(jnp.int32, shape, dim)


def place(y, zl, x, zh, core):
    return (lax.rem(y, 4) * 8 + lax.rem(zl, 2) * 4 + lax.rem(x, 4), lax.rem(zh, 4) * 2 + core)


def inverse_lanes(shape):
    index = lax.rem(iota(shape, 1), 32)
    out = jnp.zeros(shape, jnp.float32)
    for j, value in enumerate(INVERSE):
        out = jnp.where(index == j, value, out)
    return out


def cos_sin(angle):
    turns = jnp.floor(angle * 0.6366197723675814 + 0.5)
    rest = angle - turns * 1.5703125
    rest = rest - turns * 4.837512969970703125e-4
    rest = rest - turns * 7.54978995489188216e-8
    z = rest * rest
    sine = rest + rest * z * (
        -1.6666654611e-1 + z * (8.3321608736e-3 - z * 1.9515295891e-4)
    )
    cosine = 1.0 - 0.5 * z + z * z * (
        4.166664568298827e-2 + z * (-1.388731625493765e-3 + z * 2.443315711809948e-5)
    )
    quadrant = turns.astype(jnp.int32) & 3
    swap = (quadrant & 1) == 1
    c = jnp.where(swap, sine, cosine)
    s = jnp.where(swap, cosine, sine)
    c = jnp.where((quadrant == 1) | (quadrant == 2), -c, c)
    s = jnp.where(quadrant >= 2, -s, s)
    return c, s


def turn(values, cosine, signed_sine):
    first = lax.rem(iota(values.shape, 1), 64) < 32
    partner = jnp.where(first, pltpu.roll(values, 96, 1), pltpu.roll(values, 32, 1))
    return values * cosine + partner * signed_sine


def sign_sine(sine):
    return jnp.where(lax.rem(iota(sine.shape, 1), 64) < 32, -sine, sine)


def nat_of(k):
    return lax.div(lax.rem(k, 64), 16) * 32 + lax.div(k, 64) * 16 + lax.rem(k, 16)


def kernel(
    qn_hbm, qr_hbm, kl_hbm, doc_hbm, off_hbm, own_hbm, wk_hbm, wv_hbm,
    out_hbm, cache_ref,
    qn, qr, kl, doc_ref, off_ref, own_ref, wk, wv, raw, keys, query, acc, top, total, mask, cos_t, sin_t, cos_p, sin_p, raw_p,
    s1, r1, s2, r2, strip, hq_out, hout, hin, out_v,
    local_sem, pa_send, pa_recv, raw_send, raw_recv, m_send, m_recv, sib_send, sib_recv,
    c1_send, c1_recv, c2_send, c2_recv, h_send, h_recv,
):
    ctx = lax.axis_index("ctx")
    head = lax.axis_index("head")
    y, zl, x = lax.div(ctx, 8), lax.rem(lax.div(ctx, 4), 2), lax.rem(ctx, 4)
    zh, core = lax.div(head, 2), lax.rem(head, 2)
    odd = lax.rem(y, 2) == 1
    even = lax.rem(y, 2) == 0
    lane_group = zl * 4 + x

    z_up = lax.rem(zh * 2 + zl + 1, 8)
    z_down = lax.rem(zh * 2 + zl + 7, 8)
    to_z_up = place(y, lax.rem(z_up, 2), x, lax.div(z_up, 2), core)
    to_z_down = place(y, lax.rem(z_down, 2), x, lax.div(z_down, 2), core)
    to_x_up = place(y, zl, x + 1, zh, core)
    to_x_down = place(y, zl, x + 3, zh, core)
    to_x_across = place(y, zl, x + 2, zh, core)
    to_y_up = place(y + 1, zl, x, zh, core)
    sibling = (ctx, zh * 2 + 1 - core)
    z_peers = []
    for d in range(1, 8):
        z = lax.rem(zh * 2 + zl + d, 8)
        z_peers.append(place(y, lax.rem(z, 2), x, lax.div(z, 2), core))
    y_peers = [place(y + d, zl, x, zh, core) for d in (1, 2, 3)]
    group_peers = []
    for d in range(1, 8):
        j = lax.rem(lane_group + d, 8)
        group_peers.append(place(y, lax.div(j, 4), lax.rem(j, 4), zh, core))
    barrier = pltpu.get_barrier_semaphore()
    greeted = z_peers + y_peers + group_peers[:3] + group_peers[4:] + [sibling]
    for peer in greeted:
        pl.semaphore_signal(barrier, inc=1, device_id=peer, device_id_type=MESH)

    locals_ = [
        pltpu.make_async_copy(kl_hbm, kl, local_sem.at[0]),
        pltpu.make_async_copy(qr_hbm, qr, local_sem.at[1]),
        pltpu.make_async_copy(qn_hbm, qn, local_sem.at[2]),
        pltpu.make_async_copy(wk_hbm, wk, local_sem.at[3]),
        pltpu.make_async_copy(wv_hbm, wv, local_sem.at[4]),
        pltpu.make_async_copy(doc_hbm, doc_ref, local_sem.at[5]),
        pltpu.make_async_copy(own_hbm, own_ref, local_sem.at[6]),
        pltpu.make_async_copy(off_hbm, off_ref, local_sem.at[7]),
    ]
    for number in (5, 6, 0, 7, 1, 2, 3, 4):
        locals_[number].start()
    lane128 = iota((TOK, 128), 1)

    @pl.when(even)
    def _():
        blank = jnp.where(iota((HALF, 128), 1) == GONE, 1.0, 0.0).astype(jnp.bfloat16)
        zero = jnp.zeros((HALF, LATENT), jnp.bfloat16)
        for scheme in (0, 1):
            for pos, (_, g) in enumerate(ORDER):
                if g >= 2:
                    keys[pos, scheme, :, :LATENT] = zero
                    keys[pos, scheme, :, LATENT:] = blank

    @pl.when(ctx != 8)
    def _():
        query[HEADS * TOK :, :] = jnp.zeros((EXTRA, WIDE), jnp.bfloat16)

    top[HEADS * TOK :, :] = jnp.zeros((EXTRA, 128), jnp.float32)
    total[HEADS * TOK :, :] = jnp.zeros((EXTRA, 128), jnp.float32)
    acc[HEADS * TOK :, :] = jnp.zeros((EXTRA, LATENT), jnp.float32)
    rest = TOK - STRIP
    strip[STRIP:, :LATENT] = jnp.zeros((rest, LATENT), jnp.bfloat16)
    strip[STRIP:, LATENT:] = jnp.where(iota((rest, 128), 1) == GONE, 1.0, 0.0).astype(jnp.bfloat16)
    inverse = inverse_lanes((8, 128))[0:1, :]
    token = (ctx * TOK + iota((TOK, 128), 0)).astype(jnp.float32)
    c, s = cos_sin(token * inverse)
    cos_t[...] = c
    sin_t[...] = sign_sine(s)
    other = y * 8 + (1 - zl) * 4 + x
    k = iota((HALF, 128), 0)
    at = other * TOK + lax.div(k, 16) * 32 + core * 16 + lax.rem(k, 16)
    c, s = cos_sin(at.astype(jnp.float32) * inverse)
    cos_p[...] = c
    sin_p[...] = sign_sine(s)
    mask[...] = jnp.where(nat_of(lane128) > iota((TOK, 128), 0), DEAD, 0.0)

    for number in (5, 6, 7):
        locals_[number].wait()
    docs = jnp.zeros((STRIP, 128), jnp.int32)
    owners = docs
    for r in range(STRIP):
        docs = jnp.where(iota((STRIP, 128), 0) == r, doc_ref[r], docs)
        owners = jnp.where(iota((STRIP, 128), 0) == r, own_ref[r], owners)
    lane = iota((STRIP, 128), 1)
    locals_[0].wait()
    facts = jnp.where((lane == DOC + docs) | (lane == COUNT + docs), 1.0, 0.0)
    facts = jnp.where(lane == BLOCK + lax.rem(ctx, 16), 1.0, facts)
    facts = jnp.where(lane == NAT, (head * STRIP + iota((STRIP, 128), 0)).astype(jnp.float32), facts)
    facts = jnp.where(lane == OWNER, owners.astype(jnp.float32), facts)
    mine = pl.ds(pl.multiple_of(zh * STRIP, STRIP), STRIP)
    raw[core, mine, :LATENT] = kl[:, :LATENT]
    raw[core, mine, LATENT:] = jnp.concatenate(
        [kl[:, LATENT:], facts[:, ROPE:].astype(jnp.bfloat16)], 1
    )
    pl.semaphore_wait(barrier, len(greeted))

    pa = [
        pltpu.make_async_remote_copy(
            src_ref=raw.at[core, mine],
            dst_ref=raw.at[core, mine] if d % 2 == 0 else raw_p.at[mine],
            send_sem=pa_send.at[d - 1], recv_sem=pa_recv.at[d - 1],
            device_id=z_peers[d - 1], device_id_type=MESH,
        )
        for d in range(1, 8)
    ]
    for d in (4, 2, 6, 3, 5, 1, 7):
        pa[d - 1].start()

    locals_[1].wait()
    for pair in range(4):
        v = turn(qr[:, pair * 128 : pair * 128 + 128].astype(jnp.float32), cos_t[...], sin_t[...])
        base = pair * 2 * TOK
        query[base : base + TOK, LATENT:] = v.astype(jnp.bfloat16)
        query[base + TOK : base + 2 * TOK, LATENT:] = pltpu.roll(v, 64, 1).astype(jnp.bfloat16)
    locals_[2].wait()
    locals_[3].wait()
    for h in range(HEADS):
        a = lax.dot_general(
            qn[:, h * NOPE : (h + 1) * NOPE], wk[h], NN, preferred_element_type=jnp.float32
        )
        query[h * TOK : (h + 1) * TOK, :LATENT] = a.astype(jnp.bfloat16)

    plan = {0: {}, 1: {}}

    def send(scheme, src, dst, to, sem):
        return pltpu.make_async_remote_copy(
            src_ref=keys.at[src, scheme], dst_ref=keys.at[dst, scheme],
            send_sem=m_send.at[sem], recv_sem=m_recv.at[dst], device_id=to, device_id_type=MESH,
        )

    def go(scheme, src, dst, to, cond=None, inside=None):
        src, dst = ORDER.index(src), ORDER.index(dst)
        make = functools.partial(send, scheme, src, dst, to, len(plan[scheme]))
        plan[scheme][src, dst, cond is None] = (make, cond if inside is None else inside)
        if cond is None:
            make().start()
        else:
            @pl.when(cond)
            def _():
                make().start()

    def arrived(scheme, pos):
        ref = keys.at[pos, scheme]
        pltpu.make_async_copy(ref, ref, m_recv.at[pos]).wait()

    def share(scheme, pos):
        return pltpu.make_async_remote_copy(
            src_ref=keys.at[pos, scheme], dst_ref=keys.at[pos, scheme],
            send_sem=sib_send.at[pos], recv_sem=sib_recv.at[pos],
            device_id=sibling, device_id_type=MESH,
        )

    def fill(scheme, pos, rows, cc, ss):
        v = rows[:, LATENT:].astype(jnp.float32)
        rotated = jnp.where(iota((HALF, 128), 1) < ROPE, turn(v, cc, ss), v)
        keys[pos, scheme, :, :LATENT] = rows[:, :LATENT]
        keys[pos, scheme, :, LATENT:] = rotated.astype(jnp.bfloat16)

    def own_slot(half):
        cc = jnp.concatenate([cos_t[n * 32 + half * 16 : n * 32 + half * 16 + 16, :] for n in range(4)], 0)
        ss = jnp.concatenate([sin_t[n * 32 + half * 16 : n * 32 + half * 16 + 16, :] for n in range(4)], 0)
        fill(half, 0, raw[half], cc, ss)

    for d in (2, 4, 6):
        pa[d - 1].wait_recv()
    share_raw = pltpu.make_async_remote_copy(
        src_ref=raw.at[core], dst_ref=raw.at[core], send_sem=raw_send, recv_sem=raw_recv,
        device_id=sibling, device_id_type=MESH,
    )
    share_raw.start()

    on_a, on_b = core == 0, core == 1

    @pl.when(on_a)
    def _():
        own_slot(0)
        go(0, (0, 0), (0, 2), to_y_up, cond=even)

    @pl.when(on_b)
    def _():
        own_slot(1)
        go(1, (0, 0), (1, 0), to_x_up)
        go(1, (0, 0), (2, 0), to_x_down)
        go(1, (0, 0), (3, 0), to_x_across)

    for d in (1, 3, 5, 7):
        pa[d - 1].wait_recv()

    @pl.when(on_a)
    def _():
        fill(0, 1, raw_p[...], cos_p[...], sin_p[...])
        go(0, (0, 1), (0, 3), to_y_up, cond=even)
        go(0, (0, 0), (1, 0), to_x_up)
        go(0, (0, 0), (2, 0), to_x_down)
        go(0, (0, 0), (3, 0), to_x_across)
        share(0, 1).start()

    @pl.when(on_b)
    def _():
        fill(1, 1, raw_p[...], cos_p[...], sin_p[...])
        go(1, (0, 0), (0, 2), to_y_up, cond=even)
        go(1, (0, 1), (0, 3), to_y_up, cond=even)
        share(1, 1).start()

    pltpu.make_async_copy(raw.at[1 - core], raw.at[1 - core], raw_recv).wait()

    @pl.when(on_a)
    def _():
        own_slot(1)

    @pl.when(on_b)
    def _():
        own_slot(0)

    bound = jnp.where(
        (lane128 == GONE)
        | ((lane128 >= BLOCK) & (lane128 < BLOCK + 16) & (lane128 - BLOCK > lax.rem(ctx, 16))),
        -BIG,
        0.0,
    )
    hot = jnp.concatenate(
        [raw[n % 2, (n // 2) * 16 : (n // 2) * 16 + 16, LATENT:] for n in range(8)], 0
    ).astype(jnp.float32)
    bound = jnp.where((lane128 >= DOC) & (lane128 < DOC + 4), (hot - 1.0) * BIG, bound)
    bound = bound.astype(jnp.bfloat16)
    for h in range(HEADS):
        rows = slice(h * TOK, (h + 1) * TOK)
        query[rows, LATENT:] = jnp.where(lane128 < ROPE, query[rows, LATENT:], bound)

    asks, helps = ctx == 16, ctx == 8

    extra = slice(HEADS * TOK, HEADS * TOK + EXTRA)

    def ask(part):
        return pltpu.make_async_remote_copy(
            src_ref=hq_out.at[pl.ds(0, EXTRA) if part == 0 else pl.ds(EXTRA, STRIP)],
            dst_ref=query.at[pl.ds(HEADS * TOK, EXTRA)] if part == 0 else strip.at[pl.ds(0, STRIP)],
            send_sem=h_send.at[part], recv_sem=h_recv.at[part],
            device_id=place(1, zl, x, zh, core), device_id_type=MESH,
        )

    def answer():
        return pltpu.make_async_remote_copy(
            src_ref=hout, dst_ref=hin, send_sem=h_send.at[2], recv_sem=h_recv.at[2],
            device_id=place(2, zl, x, zh, core), device_id_type=MESH,
        )

    @pl.when(asks)
    def _():
        firsts = jnp.concatenate(
            [query[h * TOK : h * TOK + 16, :].astype(jnp.float32)[:8] for h in range(HEADS)], 0
        )
        firsts = jnp.where(iota((EXTRA, WIDE), 1) >= LATENT + BLOCK, 0.0, firsts)
        hq_out[:EXTRA, :] = firsts.astype(jnp.bfloat16)
        hq_out[EXTRA:, :] = keys[0, 0, 0:STRIP, :]
        ask(0).start()
        ask(1).start()

    my_y = pl.ds(pl.multiple_of(y * 16, 16), 16)

    def cache1(d):
        there = lax.rem(y + d, 4)
        return pltpu.make_async_remote_copy(
            src_ref=s1.at[pl.ds(pl.multiple_of(there * 16, 16), 16)], dst_ref=r1.at[my_y],
            send_sem=c1_send.at[d - 1], recv_sem=c1_recv.at[d - 1], device_id=y_peers[d - 1],
            device_id_type=MESH,
        )

    def cache_begin():
        both = raw[...].reshape(TOK, WIDE)
        pick = jnp.where(iota((8, 128), 1) == OWNER, 1.0, 0.0).astype(jnp.bfloat16)
        owner = lax.dot_general(pick, both[:, LATENT:], NT, preferred_element_type=jnp.float32)[0:1, :]
        line = iota((64, TOK), 0)
        named = jnp.where(lax.rem(line, 16) < 8, lax.div(line, 16) * 8 + lax.rem(line, 16), -1)
        hits = owner == named.astype(jnp.float32)
        hits_b = jnp.where(hits, 1.0, 0.0).astype(jnp.bfloat16)
        before = nat_of(iota((TOK, TOK), 0)) < nat_of(iota((TOK, TOK), 1))
        rank = lax.dot_general(
            hits_b, jnp.where(before, 1.0, 0.0).astype(jnp.bfloat16), NN,
            preferred_element_type=jnp.float32,
        )
        chosen = jnp.where(hits & (rank == head.astype(jnp.float32)), 1.0, 0.0).astype(jnp.bfloat16)
        rows64 = lax.dot_general(chosen, both, NN, preferred_element_type=jnp.float32)
        counts = lax.dot_general(
            jnp.ones((64, TOK), jnp.bfloat16), both[:, LATENT:], NN, preferred_element_type=jnp.float32
        )
        lane64 = iota((64, 128), 1)
        s1[:, :LATENT] = rows64[:, :LATENT].astype(jnp.bfloat16)
        s1[:, LATENT:] = jnp.where(
            (lane64 >= COUNT) & (lane64 < COUNT + 4), counts, rows64[:, LATENT:]
        ).astype(jnp.bfloat16)
        r1[my_y, :] = s1[my_y, :]
        for d in (1, 2, 3):
            cache1(d).start()

    my_group = pl.ds(pl.multiple_of(lane_group * 16, 16), 16)

    def cache2(d):
        there = lax.rem(lane_group + d, 8)
        return pltpu.make_async_remote_copy(
            src_ref=s2.at[pl.ds(pl.multiple_of(there * 16, 16), 16)], dst_ref=r2.at[my_group],
            send_sem=c2_send.at[d - 1], recv_sem=c2_recv.at[d - 1], device_id=group_peers[d - 1],
            device_id_type=MESH,
        )

    def cache_middle():
        for d in (1, 2, 3):
            cache1(d).wait_recv()
        to, source = iota((128, 64), 0), iota((128, 64), 1)
        ys, j = lax.rem(to, 16), lax.div(to, 16)
        permute = jnp.where((ys < 4) & (source == ys * 16 + j), 1.0, 0.0).astype(jnp.bfloat16)
        s2[...] = lax.dot_general(
            permute, r1[...], NN, preferred_element_type=jnp.float32
        ).astype(jnp.bfloat16)
        r2[my_group, :] = s2[my_group, :]
        for d in range(1, 8):
            cache2(d).start()

    def cache_end():
        for d in range(1, 8):
            cache2(d).wait_recv()
        slot, source = iota((32, 128), 0), iota((32, 128), 1)
        permute = jnp.where(
            source == lax.rem(slot, 8) * 16 + lax.div(slot, 8), 1.0, 0.0
        ).astype(jnp.bfloat16)
        rows = lax.dot_general(permute, r2[...], NN, preferred_element_type=jnp.float32)
        facts = rows[:, LATENT:]
        lane32 = iota((32, 128), 1)
        sums = jnp.sum(facts, 0, keepdims=True)
        lane1 = iota((1, 128), 1)

        def lane_of(values, index, at):
            return jnp.sum(jnp.where(at == index, values, 0.0), 1, keepdims=True)

        number = sum(d * lane_of(facts, DOC + d, lane32) for d in (1, 2, 3))
        start = sum(
            jnp.where(number > d, lane_of(sums, COUNT + d, lane1), 0.0) for d in range(3)
        )
        offset = jnp.zeros((32, 1), jnp.float32)
        for d in range(4):
            offset = jnp.where(number == d, off_ref[d].astype(jnp.float32), offset)
        at = (iota((32, 1), 0) * TOK).astype(jnp.float32) + lane_of(facts, NAT, lane32)
        c, s = cos_sin((offset + at - start) * inverse)
        turned = turn(facts, c, sign_sine(s))
        cache_ref[:, :LATENT] = rows[:, :LATENT].astype(jnp.bfloat16)
        cache_ref[:, LATENT:] = turned.astype(jnp.bfloat16)

    def step(pos):
        xr, g = here = ORDER[pos]
        inside = None if g < 2 else odd

        @pl.when(on_a if g < 2 else on_a & odd)
        def _():
            arrived(0, pos)
            if xr == 0:
                go(0, here, (1, g), to_x_up, inside=inside)
                go(0, here, (2, g), to_x_down, inside=inside)
                go(0, here, (3, g), to_x_across, inside=inside)
            if g == 0:
                go(0, here, (xr, 1), to_z_up if xr == 1 else to_z_down)
            share(0, pos).start()

        @pl.when(on_b if g < 2 else on_b & odd)
        def _():
            arrived(1, pos)
            if g == 0:
                go(1, here, (xr, 2), to_y_up, cond=even)
                go(1, here, (xr, 1), to_z_down if xr == 2 else to_z_up)
            if g == 2 and xr > 0:
                go(1, here, (xr, 3), to_z_up if xr == 1 else to_z_down, inside=odd)
            share(1, pos).start()

    def shared(chunk):
        for pos in range(*CHUNKS[chunk]):
            if pos == 0:
                continue

            @pl.when(on_a if ORDER[pos][1] < 2 else on_a & odd)
            def _():
                share(1, pos).wait_recv()

            @pl.when(on_b if ORDER[pos][1] < 2 else on_b & odd)
            def _():
                share(0, pos).wait_recv()

    def rows_of(chunk):
        first, end = CHUNKS[chunk]
        return keys[first:end].reshape((end - first) * TOK, WIDE)

    def scores(q, k):
        return lax.dot_general(q, k, NT, preferred_element_type=jnp.float32) * SCALE

    def absorb(p, values, rows, first):
        size = rows.stop - rows.start
        most = jnp.max(p, 1, keepdims=True)
        if not first:
            old = top[rows, 0:1]
            most = jnp.maximum(old, most)
            shrink = jnp.exp2(old - most)
        weights = jnp.exp2(p - most)
        added = sum(weights[:, n * 128 : (n + 1) * 128] for n in range(p.shape[1] // 128))
        top[rows, :] = jnp.broadcast_to(most, (size, 128))
        total[rows, :] = added if first else total[rows, :] * shrink + added
        mixed = lax.dot_general(
            weights.astype(jnp.bfloat16), values, NN, preferred_element_type=jnp.float32
        )
        acc[rows, :] = mixed if first else acc[rows, :] * shrink + mixed

    count = HEADS * TOK // TILE
    tiles = [slice(i * TILE, (i + 1) * TILE) for i in range(count)]
    wide_tiles = tiles[:-1] + [slice(tiles[-1].start, extra.stop)]

    def tile(chunk, rows, p):
        if chunk == 0:
            own_part = p[:, :TOK].reshape(TILE // TOK, TOK, TOK) + mask[...][None]
            p = jnp.concatenate([own_part.reshape(TILE, TOK), p[:, TOK:]], 1)
        absorb(p, rows_of(chunk)[:, :LATENT], rows, chunk == 0)

    def sweep(chunk, order, after_first=None):
        p = scores(query[order[0], :], rows_of(chunk))
        for i, rows in enumerate(order):
            following = None
            if i + 1 < len(order):
                following = scores(query[order[i + 1], :], rows_of(chunk))
            tile(chunk, rows, p)
            p = following
            if i == 0 and after_first is not None:
                after_first()

    def help_first():
        ask(0).wait_recv()
        ask(1).wait_recv()
        p = scores(query[extra, :], strip[...])
        p = jnp.where(iota((EXTRA, TOK), 1) <= lax.rem(iota((EXTRA, TOK), 0), 8), p, DEAD)
        absorb(p, strip[:, :LATENT], extra, True)
        absorb(scores(query[extra, :], rows_of(0)), rows_of(0)[:, :LATENT], extra, False)

    def help_last():
        hout[...] = (acc[extra, :] / jnp.sum(total[extra, :], 1, keepdims=True)).astype(
            jnp.bfloat16
        )
        answer().start()

    cache_begin()
    shared(0)
    sweep(0, tiles)
    for pos in range(2, 6):
        step(pos)

    @pl.when(helps)
    def _():
        help_first()

    cache_middle()
    shared(1)
    sweep(1, wide_tiles)
    for pos in range(6, 13):
        step(pos)
    shared(2)

    @pl.when(helps)
    def _():
        sweep(2, [extra])

    @pl.when(jnp.logical_not(helps))
    def _():
        sweep(2, tiles)

    step(13)
    shared(3)
    sweep(3, wide_tiles)
    step(14)
    step(15)
    cache_end()
    shared(4)
    sweep(4, wide_tiles[::-1], lambda: pl.when(helps)(help_last))

    @pl.when(asks)
    def _():
        answer().wait_recv()
        theirs = hin[...].astype(jnp.float32)
        for h in range(HEADS):
            rows = slice(h * TOK, h * TOK + 8)
            acc[rows, :] = theirs[h * 8 : (h + 1) * 8]
            total[rows, :] = jnp.where(iota((8, 128), 1) == 0, 1.0, 0.0)

    locals_[4].wait()

    def store(part):
        columns = pl.ds(part * 4 * VDIM, 4 * VDIM)
        return pltpu.make_async_copy(
            out_v.at[:, columns], out_hbm.at[:, columns], local_sem.at[part]
        )

    for h in range(HEADS):
        rows = slice(h * TOK, (h + 1) * TOK)
        share_of = 1.0 / jnp.sum(total[rows, :], 1, keepdims=True)
        latent = (acc[rows, :] * share_of).astype(jnp.bfloat16)
        out_v[:, h * VDIM : (h + 1) * VDIM] = lax.dot_general(
            latent, wv[h], NN, preferred_element_type=jnp.float32
        ).astype(jnp.bfloat16)
        if h % 4 == 3:
            store(h // 4).start()

    store(0).wait()
    store(1).wait()
    for copy in pa:
        copy.wait_send()
    share_raw.wait_send()
    for scheme, on in ((0, on_a), (1, on_b)):
        @pl.when(on)
        def _():
            for make, cond in plan[scheme].values():
                if cond is None:
                    make().wait_send()
                else:
                    @pl.when(cond)
                    def _():
                        make().wait_send()
            for pos in range(1, 16):
                if ORDER[pos][1] < 2:
                    share(scheme, pos).wait_send()
                else:
                    @pl.when(odd)
                    def _():
                        share(scheme, pos).wait_send()
    for d in (1, 2, 3):
        cache1(d).wait_send()
    for d in range(1, 8):
        cache2(d).wait_send()

    @pl.when(asks)
    def _():
        ask(0).wait_send()
        ask(1).wait_send()

    @pl.when(helps)
    def _():
        answer().wait_send()


def local(q_nope, q_rope, key_latent, doc_ids, doc_offsets, owners, w_key, w_value):
    bf, f32 = jnp.bfloat16, jnp.float32
    vmem = pltpu.VMEM
    dma = pltpu.SemaphoreType.DMA
    hbm = pl.BlockSpec(memory_space=pl.ANY)
    smem = pltpu.SMEM
    rows = HEADS * TOK
    operands = (
        q_nope, q_rope, key_latent, doc_ids, doc_offsets, owners.reshape(STRIP), w_key, w_value
    )
    operands = [pltpu.with_memory_space_constraint(a, pltpu.HBM) for a in operands]
    attended, cache = pl.pallas_call(
        kernel,
        out_shape=(
            jax.ShapeDtypeStruct((TOK, HEADS * VDIM), bf),
            jax.ShapeDtypeStruct((32, WIDE), bf),
        ),
        in_specs=[hbm] * 8,
        out_specs=(hbm, pl.BlockSpec(memory_space=vmem)),
        scratch_shapes=[
            vmem((TOK, HEADS * NOPE), bf),
            vmem((TOK, HEADS * ROPE), bf),
            vmem((STRIP, LATENT + ROPE), bf),
            smem((STRIP,), jnp.int32),
            smem((4,), jnp.int32),
            smem((STRIP,), jnp.int32),
            vmem((HEADS, NOPE, LATENT), bf),
            vmem((HEADS, LATENT, VDIM), bf),
            vmem((2, HALF, WIDE), bf),
            vmem((16, 2, HALF, WIDE), bf),
            vmem((rows + EXTRA, WIDE), bf),
            vmem((rows + EXTRA, LATENT), f32),
            vmem((rows + EXTRA, 128), f32),
            vmem((rows + EXTRA, 128), f32),
            vmem((TOK, 128), f32),
            vmem((TOK, 128), f32),
            vmem((TOK, 128), f32),
            vmem((HALF, 128), f32),
            vmem((HALF, 128), f32),
            vmem((HALF, WIDE), bf),
            vmem((64, WIDE), bf),
            vmem((64, WIDE), bf),
            vmem((128, WIDE), bf),
            vmem((128, WIDE), bf),
            vmem((TOK, WIDE), bf),
            vmem((EXTRA + STRIP, WIDE), bf),
            vmem((EXTRA, LATENT), bf),
            vmem((EXTRA, LATENT), bf),
            vmem((TOK, HEADS * VDIM), bf),
            dma((8,)),
            dma((7,)),
            dma((7,)),
            dma,
            dma,
            dma((24,)),
            dma((16,)),
            dma((16,)),
            dma((16,)),
            dma((3,)),
            dma((3,)),
            dma((7,)),
            dma((7,)),
            dma((3,)),
            dma((3,)),
        ],
        compiler_params=pltpu.CompilerParams(
            collective_id=0, has_side_effects=True, vmem_limit_bytes=40 * 2**20
        ),
        name="latent_attention",
    )(*operands)
    return attended, cache[:, : LATENT + ROPE]


def solution(mesh):
    in_specs = (
        P("ctx", "head"),
        P("ctx", "head"),
        P(("ctx", "head"), None),
        P(("ctx", "head")),
        P(),
        P(("ctx", "head"), None),
        P("head", None, None),
        P("head", None, None),
    )
    out_specs = (P("ctx", "head"), P(("ctx", "head"), None))
    return jax.shard_map(local, mesh=mesh, in_specs=in_specs, out_specs=out_specs, check_vma=False)
```

```python
import functools

import jax
import jax.numpy as jnp
import numpy as np
from jax import lax
from jax.experimental import pallas as pl
from jax.experimental.pallas import tpu as pltpu
from jax.sharding import PartitionSpec as P

NOPE = 128
ROPE = 64
LATENT = 512
VDIM = 128
HEADS = 8
TOK = 128
HALF = 64
WIDE = 640
STRIP = 16
TILE = 256
BIG = float(2.0**100)
DEAD = -1e30
SCALE = (NOPE + ROPE) ** -0.5 * 1.4426950408889634
INVERSE = [float(v) for v in (10000.0 ** (-2.0 * np.arange(32) / 64.0)).astype(np.float32)]
DOC = 64
GONE = 68
NAT = 69
OWNER = 70
COUNT = 72
BLOCK = 80
EXTRA = 64

ORDER = (
    (0, 0), (0, 1), (1, 0), (2, 0), (0, 2), (0, 3), (3, 0), (1, 1),
    (2, 1), (3, 1), (1, 2), (2, 2), (3, 2), (1, 3), (2, 3), (3, 3),
)
CHUNKS = ((0, 2), (2, 6), (6, 10), (10, 14), (14, 16))

MESH = pl.DeviceIdType.MESH
NT = (((1,), (1,)), ((), ()))
NN = (((1,), (0,)), ((), ()))


def iota(shape, dim):
    return lax.broadcasted_iota(jnp.int32, shape, dim)


def place(y, zl, x, zh, core):
    return (lax.rem(y, 4) * 8 + lax.rem(zl, 2) * 4 + lax.rem(x, 4), lax.rem(zh, 4) * 2 + core)


def inverse_lanes(shape):
    index = lax.rem(iota(shape, 1), 32)
    out = jnp.zeros(shape, jnp.float32)
    for j, value in enumerate(INVERSE):
        out = jnp.where(index == j, value, out)
    return out


def cos_sin(angle):
    turns = jnp.floor(angle * 0.6366197723675814 + 0.5)
    rest = angle - turns * 1.5703125
    rest = rest - turns * 4.837512969970703125e-4
    rest = rest - turns * 7.54978995489188216e-8
    z = rest * rest
    sine = rest + rest * z * (
        -1.6666654611e-1 + z * (8.3321608736e-3 - z * 1.9515295891e-4)
    )
    cosine = 1.0 - 0.5 * z + z * z * (
        4.166664568298827e-2 + z * (-1.388731625493765e-3 + z * 2.443315711809948e-5)
    )
    quadrant = turns.astype(jnp.int32) & 3
    swap = (quadrant & 1) == 1
    c = jnp.where(swap, sine, cosine)
    s = jnp.where(swap, cosine, sine)
    c = jnp.where((quadrant == 1) | (quadrant == 2), -c, c)
    s = jnp.where(quadrant >= 2, -s, s)
    return c, s


def turn(values, cosine, signed_sine):
    first = lax.rem(iota(values.shape, 1), 64) < 32
    partner = jnp.where(first, pltpu.roll(values, 96, 1), pltpu.roll(values, 32, 1))
    return values * cosine + partner * signed_sine


def sign_sine(sine):
    return jnp.where(lax.rem(iota(sine.shape, 1), 64) < 32, -sine, sine)


def nat_of(k):
    return lax.div(lax.rem(k, 64), 16) * 32 + lax.div(k, 64) * 16 + lax.rem(k, 16)


def kernel(
    qn_hbm, qr_hbm, kl_hbm, doc_hbm, off_hbm, own_hbm, wk_hbm, wv_hbm,
    out_hbm, cache_ref,
    qn, qr, kl, doc_ref, off_ref, own_ref, wk, wv, raw, keys, query, acc, top, total, mask, cos_t, sin_t, cos_p, sin_p, raw_p,
    s1, r1, s2, r2, strip, hq_out, hout, hin, out_v,
    local_sem, pa_send, pa_recv, raw_send, raw_recv, m_send, m_recv, sib_send, sib_recv,
    c1_send, c1_recv, c2_send, c2_recv, h_send, h_recv,
):
    ctx = lax.axis_index("ctx")
    head = lax.axis_index("head")
    y, zl, x = lax.div(ctx, 8), lax.rem(lax.div(ctx, 4), 2), lax.rem(ctx, 4)
    zh, core = lax.div(head, 2), lax.rem(head, 2)
    odd = lax.rem(y, 2) == 1
    even = lax.rem(y, 2) == 0
    lane_group = zl * 4 + x

    z_up = lax.rem(zh * 2 + zl + 1, 8)
    z_down = lax.rem(zh * 2 + zl + 7, 8)
    to_z_up = place(y, lax.rem(z_up, 2), x, lax.div(z_up, 2), core)
    to_z_down = place(y, lax.rem(z_down, 2), x, lax.div(z_down, 2), core)
    to_x_up = place(y, zl, x + 1, zh, core)
    to_x_down = place(y, zl, x + 3, zh, core)
    to_x_across = place(y, zl, x + 2, zh, core)
    to_y_up = place(y + 1, zl, x, zh, core)
    sibling = (ctx, zh * 2 + 1 - core)
    z_peers = []
    for d in range(1, 8):
        z = lax.rem(zh * 2 + zl + d, 8)
        z_peers.append(place(y, lax.rem(z, 2), x, lax.div(z, 2), core))
    y_peers = [place(y + d, zl, x, zh, core) for d in (1, 2, 3)]
    group_peers = []
    for d in range(1, 8):
        j = lax.rem(lane_group + d, 8)
        group_peers.append(place(y, lax.div(j, 4), lax.rem(j, 4), zh, core))
    barrier = pltpu.get_barrier_semaphore()
    greeted = z_peers + y_peers + group_peers[:3] + group_peers[4:] + [sibling]
    for peer in greeted:
        pl.semaphore_signal(barrier, inc=1, device_id=peer, device_id_type=MESH)

    locals_ = [
        pltpu.make_async_copy(kl_hbm, kl, local_sem.at[0]),
        pltpu.make_async_copy(qr_hbm, qr, local_sem.at[1]),
        pltpu.make_async_copy(qn_hbm, qn, local_sem.at[2]),
        pltpu.make_async_copy(wk_hbm, wk, local_sem.at[3]),
        pltpu.make_async_copy(wv_hbm, wv, local_sem.at[4]),
        pltpu.make_async_copy(doc_hbm, doc_ref, local_sem.at[5]),
        pltpu.make_async_copy(own_hbm, own_ref, local_sem.at[6]),
        pltpu.make_async_copy(off_hbm, off_ref, local_sem.at[7]),
    ]
    for number in (5, 6, 0, 7, 1, 2, 3, 4):
        locals_[number].start()
    lane128 = iota((TOK, 128), 1)

    @pl.when(even)
    def _():
        blank = jnp.where(iota((HALF, 128), 1) == GONE, 1.0, 0.0).astype(jnp.bfloat16)
        zero = jnp.zeros((HALF, LATENT), jnp.bfloat16)
        for scheme in (0, 1):
            for pos, (_, g) in enumerate(ORDER):
                if g >= 2:
                    keys[pos, scheme, :, :LATENT] = zero
                    keys[pos, scheme, :, LATENT:] = blank

    @pl.when(ctx != 8)
    def _():
        query[HEADS * TOK :, :] = jnp.zeros((EXTRA, WIDE), jnp.bfloat16)

    top[HEADS * TOK :, :] = jnp.zeros((EXTRA, 128), jnp.float32)
    total[HEADS * TOK :, :] = jnp.zeros((EXTRA, 128), jnp.float32)
    acc[HEADS * TOK :, :] = jnp.zeros((EXTRA, LATENT), jnp.float32)
    rest = TOK - STRIP
    strip[STRIP:, :LATENT] = jnp.zeros((rest, LATENT), jnp.bfloat16)
    strip[STRIP:, LATENT:] = jnp.where(iota((rest, 128), 1) == GONE, 1.0, 0.0).astype(jnp.bfloat16)
    inverse = inverse_lanes((8, 128))[0:1, :]
    token = (ctx * TOK + iota((TOK, 128), 0)).astype(jnp.float32)
    c, s = cos_sin(token * inverse)
    cos_t[...] = c
    sin_t[...] = sign_sine(s)
    other = y * 8 + (1 - zl) * 4 + x
    k = iota((HALF, 128), 0)
    at = other * TOK + lax.div(k, 16) * 32 + core * 16 + lax.rem(k, 16)
    c, s = cos_sin(at.astype(jnp.float32) * inverse)
    cos_p[...] = c
    sin_p[...] = sign_sine(s)
    mask[...] = jnp.where(nat_of(lane128) > iota((TOK, 128), 0), DEAD, 0.0)

    for number in (5, 6, 7):
        locals_[number].wait()
    docs = jnp.zeros((STRIP, 128), jnp.int32)
    owners = docs
    for r in range(STRIP):
        docs = jnp.where(iota((STRIP, 128), 0) == r, doc_ref[r], docs)
        owners = jnp.where(iota((STRIP, 128), 0) == r, own_ref[r], owners)
    lane = iota((STRIP, 128), 1)
    locals_[0].wait()
    facts = jnp.where((lane == DOC + docs) | (lane == COUNT + docs), 1.0, 0.0)
    facts = jnp.where(lane == BLOCK + lax.rem(ctx, 16), 1.0, facts)
    facts = jnp.where(lane == NAT, (head * STRIP + iota((STRIP, 128), 0)).astype(jnp.float32), facts)
    facts = jnp.where(lane == OWNER, owners.astype(jnp.float32), facts)
    mine = pl.ds(pl.multiple_of(zh * STRIP, STRIP), STRIP)
    raw[core, mine, :LATENT] = kl[:, :LATENT]
    raw[core, mine, LATENT:] = jnp.concatenate(
        [kl[:, LATENT:], facts[:, ROPE:].astype(jnp.bfloat16)], 1
    )
    pl.semaphore_wait(barrier, len(greeted))

    pa = [
        pltpu.make_async_remote_copy(
            src_ref=raw.at[core, mine],
            dst_ref=raw.at[core, mine] if d % 2 == 0 else raw_p.at[mine],
            send_sem=pa_send.at[d - 1], recv_sem=pa_recv.at[d - 1],
            device_id=z_peers[d - 1], device_id_type=MESH,
        )
        for d in range(1, 8)
    ]
    for d in (4, 2, 6, 3, 5, 1, 7):
        pa[d - 1].start()

    locals_[1].wait()
    for pair in range(4):
        v = turn(qr[:, pair * 128 : pair * 128 + 128].astype(jnp.float32), cos_t[...], sin_t[...])
        base = pair * 2 * TOK
        query[base : base + TOK, LATENT:] = v.astype(jnp.bfloat16)
        query[base + TOK : base + 2 * TOK, LATENT:] = pltpu.roll(v, 64, 1).astype(jnp.bfloat16)
    locals_[2].wait()
    locals_[3].wait()
    for h in range(HEADS):
        a = lax.dot_general(
            qn[:, h * NOPE : (h + 1) * NOPE], wk[h], NN, preferred_element_type=jnp.float32
        )
        query[h * TOK : (h + 1) * TOK, :LATENT] = a.astype(jnp.bfloat16)

    plan = {0: {}, 1: {}}

    def send(scheme, src, dst, to, sem):
        return pltpu.make_async_remote_copy(
            src_ref=keys.at[src, scheme], dst_ref=keys.at[dst, scheme],
            send_sem=m_send.at[sem], recv_sem=m_recv.at[dst], device_id=to, device_id_type=MESH,
        )

    def go(scheme, src, dst, to, cond=None, inside=None):
        src, dst = ORDER.index(src), ORDER.index(dst)
        make = functools.partial(send, scheme, src, dst, to, len(plan[scheme]))
        plan[scheme][src, dst, cond is None] = (make, cond if inside is None else inside)
        if cond is None:
            make().start()
        else:
            @pl.when(cond)
            def _():
                make().start()

    def arrived(scheme, pos):
        ref = keys.at[pos, scheme]
        pltpu.make_async_copy(ref, ref, m_recv.at[pos]).wait()

    def share(scheme, pos):
        return pltpu.make_async_remote_copy(
            src_ref=keys.at[pos, scheme], dst_ref=keys.at[pos, scheme],
            send_sem=sib_send.at[pos], recv_sem=sib_recv.at[pos],
            device_id=sibling, device_id_type=MESH,
        )

    def fill(scheme, pos, rows, cc, ss):
        v = rows[:, LATENT:].astype(jnp.float32)
        rotated = jnp.where(iota((HALF, 128), 1) < ROPE, turn(v, cc, ss), v)
        keys[pos, scheme, :, :LATENT] = rows[:, :LATENT]
        keys[pos, scheme, :, LATENT:] = rotated.astype(jnp.bfloat16)

    def own_slot(half):
        cc = jnp.concatenate([cos_t[n * 32 + half * 16 : n * 32 + half * 16 + 16, :] for n in range(4)], 0)
        ss = jnp.concatenate([sin_t[n * 32 + half * 16 : n * 32 + half * 16 + 16, :] for n in range(4)], 0)
        fill(half, 0, raw[half], cc, ss)

    for d in (2, 4, 6):
        pa[d - 1].wait_recv()
    share_raw = pltpu.make_async_remote_copy(
        src_ref=raw.at[core], dst_ref=raw.at[core], send_sem=raw_send, recv_sem=raw_recv,
        device_id=sibling, device_id_type=MESH,
    )
    share_raw.start()

    on_a, on_b = core == 0, core == 1

    @pl.when(on_a)
    def _():
        own_slot(0)
        go(0, (0, 0), (0, 2), to_y_up, cond=even)

    @pl.when(on_b)
    def _():
        own_slot(1)
        go(1, (0, 0), (1, 0), to_x_up)
        go(1, (0, 0), (2, 0), to_x_down)
        go(1, (0, 0), (3, 0), to_x_across)

    for d in (1, 3, 5, 7):
        pa[d - 1].wait_recv()

    @pl.when(on_a)
    def _():
        fill(0, 1, raw_p[...], cos_p[...], sin_p[...])
        go(0, (0, 1), (0, 3), to_y_up, cond=even)
        go(0, (0, 0), (1, 0), to_x_up)
        go(0, (0, 0), (2, 0), to_x_down)
        go(0, (0, 0), (3, 0), to_x_across)
        share(0, 1).start()

    @pl.when(on_b)
    def _():
        fill(1, 1, raw_p[...], cos_p[...], sin_p[...])
        go(1, (0, 0), (0, 2), to_y_up, cond=even)
        go(1, (0, 1), (0, 3), to_y_up, cond=even)
        share(1, 1).start()

    pltpu.make_async_copy(raw.at[1 - core], raw.at[1 - core], raw_recv).wait()

    @pl.when(on_a)
    def _():
        own_slot(1)

    @pl.when(on_b)
    def _():
        own_slot(0)

    bound = jnp.where(
        (lane128 == GONE)
        | ((lane128 >= BLOCK) & (lane128 < BLOCK + 16) & (lane128 - BLOCK > lax.rem(ctx, 16))),
        -BIG,
        0.0,
    )
    hot = jnp.concatenate(
        [raw[n % 2, (n // 2) * 16 : (n // 2) * 16 + 16, LATENT:] for n in range(8)], 0
    ).astype(jnp.float32)
    bound = jnp.where((lane128 >= DOC) & (lane128 < DOC + 4), (hot - 1.0) * BIG, bound)
    bound = bound.astype(jnp.bfloat16)
    for h in range(HEADS):
        rows = slice(h * TOK, (h + 1) * TOK)
        query[rows, LATENT:] = jnp.where(lane128 < ROPE, query[rows, LATENT:], bound)

    asks, helps = ctx == 16, ctx == 8

    extra = slice(HEADS * TOK, HEADS * TOK + EXTRA)

    def ask(part):
        return pltpu.make_async_remote_copy(
            src_ref=hq_out.at[pl.ds(0, EXTRA) if part == 0 else pl.ds(EXTRA, STRIP)],
            dst_ref=query.at[pl.ds(HEADS * TOK, EXTRA)] if part == 0 else strip.at[pl.ds(0, STRIP)],
            send_sem=h_send.at[part], recv_sem=h_recv.at[part],
            device_id=place(1, zl, x, zh, core), device_id_type=MESH,
        )

    def answer():
        return pltpu.make_async_remote_copy(
            src_ref=hout, dst_ref=hin, send_sem=h_send.at[2], recv_sem=h_recv.at[2],
            device_id=place(2, zl, x, zh, core), device_id_type=MESH,
        )

    @pl.when(asks)
    def _():
        firsts = jnp.concatenate(
            [query[h * TOK : h * TOK + 16, :].astype(jnp.float32)[:8] for h in range(HEADS)], 0
        )
        firsts = jnp.where(iota((EXTRA, WIDE), 1) >= LATENT + BLOCK, 0.0, firsts)
        hq_out[:EXTRA, :] = firsts.astype(jnp.bfloat16)
        hq_out[EXTRA:, :] = keys[0, 0, 0:STRIP, :]
        ask(0).start()
        ask(1).start()

    my_y = pl.ds(pl.multiple_of(y * 16, 16), 16)

    def cache1(d):
        there = lax.rem(y + d, 4)
        return pltpu.make_async_remote_copy(
            src_ref=s1.at[pl.ds(pl.multiple_of(there * 16, 16), 16)], dst_ref=r1.at[my_y],
            send_sem=c1_send.at[d - 1], recv_sem=c1_recv.at[d - 1], device_id=y_peers[d - 1],
            device_id_type=MESH,
        )

    def cache_begin():
        both = raw[...].reshape(TOK, WIDE)
        pick = jnp.where(iota((8, 128), 1) == OWNER, 1.0, 0.0).astype(jnp.bfloat16)
        owner = lax.dot_general(pick, both[:, LATENT:], NT, preferred_element_type=jnp.float32)[0:1, :]
        line = iota((64, TOK), 0)
        named = jnp.where(lax.rem(line, 16) < 8, lax.div(line, 16) * 8 + lax.rem(line, 16), -1)
        hits = owner == named.astype(jnp.float32)
        hits_b = jnp.where(hits, 1.0, 0.0).astype(jnp.bfloat16)
        before = nat_of(iota((TOK, TOK), 0)) < nat_of(iota((TOK, TOK), 1))
        rank = lax.dot_general(
            hits_b, jnp.where(before, 1.0, 0.0).astype(jnp.bfloat16), NN,
            preferred_element_type=jnp.float32,
        )
        chosen = jnp.where(hits & (rank == head.astype(jnp.float32)), 1.0, 0.0).astype(jnp.bfloat16)
        rows64 = lax.dot_general(chosen, both, NN, preferred_element_type=jnp.float32)
        counts = lax.dot_general(
            jnp.ones((64, TOK), jnp.bfloat16), both[:, LATENT:], NN, preferred_element_type=jnp.float32
        )
        lane64 = iota((64, 128), 1)
        s1[:, :LATENT] = rows64[:, :LATENT].astype(jnp.bfloat16)
        s1[:, LATENT:] = jnp.where(
            (lane64 >= COUNT) & (lane64 < COUNT + 4), counts, rows64[:, LATENT:]
        ).astype(jnp.bfloat16)
        r1[my_y, :] = s1[my_y, :]
        for d in (1, 2, 3):
            cache1(d).start()

    my_group = pl.ds(pl.multiple_of(lane_group * 16, 16), 16)

    def cache2(d):
        there = lax.rem(lane_group + d, 8)
        return pltpu.make_async_remote_copy(
            src_ref=s2.at[pl.ds(pl.multiple_of(there * 16, 16), 16)], dst_ref=r2.at[my_group],
            send_sem=c2_send.at[d - 1], recv_sem=c2_recv.at[d - 1], device_id=group_peers[d - 1],
            device_id_type=MESH,
        )

    def cache_middle():
        for d in (1, 2, 3):
            cache1(d).wait_recv()
        to, source = iota((128, 64), 0), iota((128, 64), 1)
        ys, j = lax.rem(to, 16), lax.div(to, 16)
        permute = jnp.where((ys < 4) & (source == ys * 16 + j), 1.0, 0.0).astype(jnp.bfloat16)
        s2[...] = lax.dot_general(
            permute, r1[...], NN, preferred_element_type=jnp.float32
        ).astype(jnp.bfloat16)
        r2[my_group, :] = s2[my_group, :]
        for d in range(1, 8):
            cache2(d).start()

    def cache_end():
        for d in range(1, 8):
            cache2(d).wait_recv()
        slot, source = iota((32, 128), 0), iota((32, 128), 1)
        permute = jnp.where(
            source == lax.rem(slot, 8) * 16 + lax.div(slot, 8), 1.0, 0.0
        ).astype(jnp.bfloat16)
        rows = lax.dot_general(permute, r2[...], NN, preferred_element_type=jnp.float32)
        facts = rows[:, LATENT:]
        lane32 = iota((32, 128), 1)
        sums = jnp.sum(facts, 0, keepdims=True)
        lane1 = iota((1, 128), 1)

        def lane_of(values, index, at):
            return jnp.sum(jnp.where(at == index, values, 0.0), 1, keepdims=True)

        number = sum(d * lane_of(facts, DOC + d, lane32) for d in (1, 2, 3))
        start = sum(
            jnp.where(number > d, lane_of(sums, COUNT + d, lane1), 0.0) for d in range(3)
        )
        offset = jnp.zeros((32, 1), jnp.float32)
        for d in range(4):
            offset = jnp.where(number == d, off_ref[d].astype(jnp.float32), offset)
        at = (iota((32, 1), 0) * TOK).astype(jnp.float32) + lane_of(facts, NAT, lane32)
        c, s = cos_sin((offset + at - start) * inverse)
        turned = turn(facts, c, sign_sine(s))
        cache_ref[:, :LATENT] = rows[:, :LATENT].astype(jnp.bfloat16)
        cache_ref[:, LATENT:] = turned.astype(jnp.bfloat16)

    def step(pos):
        xr, g = here = ORDER[pos]
        inside = None if g < 2 else odd

        @pl.when(on_a if g < 2 else on_a & odd)
        def _():
            arrived(0, pos)
            if xr == 0:
                go(0, here, (1, g), to_x_up, inside=inside)
                go(0, here, (2, g), to_x_down, inside=inside)
                go(0, here, (3, g), to_x_across, inside=inside)
            if g == 0:
                go(0, here, (xr, 1), to_z_up if xr == 1 else to_z_down)
            share(0, pos).start()

        @pl.when(on_b if g < 2 else on_b & odd)
        def _():
            arrived(1, pos)
            if g == 0:
                go(1, here, (xr, 2), to_y_up, cond=even)
                go(1, here, (xr, 1), to_z_down if xr == 2 else to_z_up)
            if g == 2 and xr > 0:
                go(1, here, (xr, 3), to_z_up if xr == 1 else to_z_down, inside=odd)
            share(1, pos).start()

    def shared(chunk):
        for pos in range(*CHUNKS[chunk]):
            if pos == 0:
                continue

            @pl.when(on_a if ORDER[pos][1] < 2 else on_a & odd)
            def _():
                share(1, pos).wait_recv()

            @pl.when(on_b if ORDER[pos][1] < 2 else on_b & odd)
            def _():
                share(0, pos).wait_recv()

    def rows_of(chunk):
        first, end = CHUNKS[chunk]
        return keys[first:end].reshape((end - first) * TOK, WIDE)

    def scores(q, k):
        return lax.dot_general(q, k, NT, preferred_element_type=jnp.float32) * SCALE

    def absorb(p, values, rows, first):
        size = rows.stop - rows.start
        most = jnp.max(p, 1, keepdims=True)
        if not first:
            old = top[rows, 0:1]
            most = jnp.maximum(old, most)
            shrink = jnp.exp2(old - most)
        weights = jnp.exp2(p - most)
        added = sum(weights[:, n * 128 : (n + 1) * 128] for n in range(p.shape[1] // 128))
        top[rows, :] = jnp.broadcast_to(most, (size, 128))
        total[rows, :] = added if first else total[rows, :] * shrink + added
        mixed = lax.dot_general(
            weights.astype(jnp.bfloat16), values, NN, preferred_element_type=jnp.float32
        )
        acc[rows, :] = mixed if first else acc[rows, :] * shrink + mixed

    count = HEADS * TOK // TILE
    tiles = [slice(i * TILE, (i + 1) * TILE) for i in range(count)]
    wide_tiles = tiles[:-1] + [slice(tiles[-1].start, extra.stop)]

    def tile(chunk, rows, p):
        if chunk == 0:
            own_part = p[:, :TOK].reshape(TILE // TOK, TOK, TOK) + mask[...][None]
            p = jnp.concatenate([own_part.reshape(TILE, TOK), p[:, TOK:]], 1)
        absorb(p, rows_of(chunk)[:, :LATENT], rows, chunk == 0)

    def sweep(chunk, order, after_first=None):
        p = scores(query[order[0], :], rows_of(chunk))
        for i, rows in enumerate(order):
            following = None
            if i + 1 < len(order):
                following = scores(query[order[i + 1], :], rows_of(chunk))
            tile(chunk, rows, p)
            p = following
            if i == 0 and after_first is not None:
                after_first()

    def help_first():
        ask(0).wait_recv()
        ask(1).wait_recv()
        p = scores(query[extra, :], strip[...])
        p = jnp.where(iota((EXTRA, TOK), 1) <= lax.rem(iota((EXTRA, TOK), 0), 8), p, DEAD)
        absorb(p, strip[:, :LATENT], extra, True)
        absorb(scores(query[extra, :], rows_of(0)), rows_of(0)[:, :LATENT], extra, False)

    def help_last():
        hout[...] = (acc[extra, :] / jnp.sum(total[extra, :], 1, keepdims=True)).astype(
            jnp.bfloat16
        )
        answer().start()

    cache_begin()
    shared(0)
    sweep(0, tiles)
    for pos in range(2, 6):
        step(pos)

    @pl.when(helps)
    def _():
        help_first()

    shared(1)
    sweep(1, wide_tiles)
    for pos in (6, 10, 11, 12, 7, 8, 9):
        step(pos)
    cache_middle()
    shared(2)

    @pl.when(helps)
    def _():
        sweep(2, [extra])

    @pl.when(jnp.logical_not(helps))
    def _():
        sweep(2, tiles)

    step(13)
    shared(3)
    sweep(3, wide_tiles)
    step(14)
    step(15)
    cache_end()
    shared(4)
    sweep(4, wide_tiles[::-1], lambda: pl.when(helps)(help_last))

    @pl.when(asks)
    def _():
        answer().wait_recv()
        theirs = hin[...].astype(jnp.float32)
        for h in range(HEADS):
            rows = slice(h * TOK, h * TOK + 8)
            acc[rows, :] = theirs[h * 8 : (h + 1) * 8]
            total[rows, :] = jnp.where(iota((8, 128), 1) == 0, 1.0, 0.0)

    locals_[4].wait()

    def store(part):
        columns = pl.ds(part * 4 * VDIM, 4 * VDIM)
        return pltpu.make_async_copy(
            out_v.at[:, columns], out_hbm.at[:, columns], local_sem.at[part]
        )

    for h in range(HEADS):
        rows = slice(h * TOK, (h + 1) * TOK)
        share_of = 1.0 / jnp.sum(total[rows, :], 1, keepdims=True)
        latent = (acc[rows, :] * share_of).astype(jnp.bfloat16)
        out_v[:, h * VDIM : (h + 1) * VDIM] = lax.dot_general(
            latent, wv[h], NN, preferred_element_type=jnp.float32
        ).astype(jnp.bfloat16)
        if h % 4 == 3:
            store(h // 4).start()

    store(0).wait()
    store(1).wait()
    for copy in pa:
        copy.wait_send()
    share_raw.wait_send()
    for scheme, on in ((0, on_a), (1, on_b)):
        @pl.when(on)
        def _():
            for make, cond in plan[scheme].values():
                if cond is None:
                    make().wait_send()
                else:
                    @pl.when(cond)
                    def _():
                        make().wait_send()
            for pos in range(1, 16):
                if ORDER[pos][1] < 2:
                    share(scheme, pos).wait_send()
                else:
                    @pl.when(odd)
                    def _():
                        share(scheme, pos).wait_send()
    for d in (1, 2, 3):
        cache1(d).wait_send()
    for d in range(1, 8):
        cache2(d).wait_send()

    @pl.when(asks)
    def _():
        ask(0).wait_send()
        ask(1).wait_send()

    @pl.when(helps)
    def _():
        answer().wait_send()


def local(q_nope, q_rope, key_latent, doc_ids, doc_offsets, owners, w_key, w_value):
    bf, f32 = jnp.bfloat16, jnp.float32
    vmem = pltpu.VMEM
    dma = pltpu.SemaphoreType.DMA
    hbm = pl.BlockSpec(memory_space=pl.ANY)
    smem = pltpu.SMEM
    rows = HEADS * TOK
    operands = (
        q_nope, q_rope, key_latent, doc_ids, doc_offsets, owners.reshape(STRIP), w_key, w_value
    )
    operands = [pltpu.with_memory_space_constraint(a, pltpu.HBM) for a in operands]
    attended, cache = pl.pallas_call(
        kernel,
        out_shape=(
            jax.ShapeDtypeStruct((TOK, HEADS * VDIM), bf),
            jax.ShapeDtypeStruct((32, WIDE), bf),
        ),
        in_specs=[hbm] * 8,
        out_specs=(hbm, pl.BlockSpec(memory_space=vmem)),
        scratch_shapes=[
            vmem((TOK, HEADS * NOPE), bf),
            vmem((TOK, HEADS * ROPE), bf),
            vmem((STRIP, LATENT + ROPE), bf),
            smem((STRIP,), jnp.int32),
            smem((4,), jnp.int32),
            smem((STRIP,), jnp.int32),
            vmem((HEADS, NOPE, LATENT), bf),
            vmem((HEADS, LATENT, VDIM), bf),
            vmem((2, HALF, WIDE), bf),
            vmem((16, 2, HALF, WIDE), bf),
            vmem((rows + EXTRA, WIDE), bf),
            vmem((rows + EXTRA, LATENT), f32),
            vmem((rows + EXTRA, 128), f32),
            vmem((rows + EXTRA, 128), f32),
            vmem((TOK, 128), f32),
            vmem((TOK, 128), f32),
            vmem((TOK, 128), f32),
            vmem((HALF, 128), f32),
            vmem((HALF, 128), f32),
            vmem((HALF, WIDE), bf),
            vmem((64, WIDE), bf),
            vmem((64, WIDE), bf),
            vmem((128, WIDE), bf),
            vmem((128, WIDE), bf),
            vmem((TOK, WIDE), bf),
            vmem((EXTRA + STRIP, WIDE), bf),
            vmem((EXTRA, LATENT), bf),
            vmem((EXTRA, LATENT), bf),
            vmem((TOK, HEADS * VDIM), bf),
            dma((8,)),
            dma((7,)),
            dma((7,)),
            dma,
            dma,
            dma((24,)),
            dma((16,)),
            dma((16,)),
            dma((16,)),
            dma((3,)),
            dma((3,)),
            dma((7,)),
            dma((7,)),
            dma((3,)),
            dma((3,)),
        ],
        compiler_params=pltpu.CompilerParams(
            collective_id=0, has_side_effects=True, vmem_limit_bytes=40 * 2**20
        ),
        name="latent_attention",
    )(*operands)
    return attended, cache[:, : LATENT + ROPE]


def solution(mesh):
    in_specs = (
        P("ctx", "head"),
        P("ctx", "head"),
        P(("ctx", "head"), None),
        P(("ctx", "head")),
        P(),
        P(("ctx", "head"), None),
        P("head", None, None),
        P("head", None, None),
    )
    out_specs = (P("ctx", "head"), P(("ctx", "head"), None))
    return jax.shard_map(local, mesh=mesh, in_specs=in_specs, out_specs=out_specs, check_vma=False)
```
